512 devices in a mesh: dp: 32 (over z_lo, y), fsdp: 16 (over x, z_hi, core).
Axes of the slice: x: 4, y: 4, z: 16 (z_hi: 2, z_lo: 8; z = z_hi * 8 + z_lo), core: 2. Of those that a mesh axis runs over, the one named last changes fastest.
Arguments:
- image_feats: bfloat16 [9216, 1536], P('dp', 'fsdp'), may hold values from -6 to 6
- image_head: bfloat16 [1536, 1536], P('fsdp'), may hold values from -0.15625 to 0.15625
- text_embed: bfloat16 [9216, 1536], P('dp', 'fsdp'), may hold values from -6 to 6
- text_ids: int32 [9216], P('dp'), may hold values from 0 to 9215, each once
- logit_scale: float32 [], replicated, may hold values from 4 to 12
- logit_bias: float32 [], replicated, may hold values from -2 to 0
Outputs:
- feature_grad: bfloat16 [9216, 1536], P('dp', 'fsdp')
- head_grad: float32 [1536, 1536], P('fsdp')
- text_grad: bfloat16 [9216, 1536], P('dp', 'fsdp')
The draws below stay inside these ranges and needn't reach their ends.
Inputs may be any that keep to these rules, and one draw needn't show every extreme that they name: `text_ids`: each of 0 to 9215 appears once.
All inputs are finite; a program needn't handle non-finite values.
Results may differ from the reference program's by a relative error of at most 0.029.
Values may be sent and summed in bfloat16 or wider, within the bound.
No kernel may reach another device: no remote copies, remote signals or barrier semaphores. Data moves between devices by JAX's collectives and lax.ppermute only.
A program may use at most 64 MiB of HBM per device.

```python
import jax
import jax.numpy as jnp
from jax import lax

W = 1536
E = 1536
B_DEV = 288
BATCH = 9216
N_DP = 32


def block_levels(rng, extent, split, smallest, top_value):
    factor_of = 1.0
    for dim, blocks in split:
        draws = jax.random.uniform(jax.random.fold_in(jax.random.fold_in(rng, 6), dim), (blocks,), jnp.float32, smallest / len(split), top_value / len(split))
        factor_of = factor_of * jnp.repeat(jnp.exp(draws), extent[dim] // blocks).reshape((-1,) + (1,) * (len(extent) - 1 - dim))
    return factor_of


def bell_draw(stream_key, extent, width, bound, shards=(), held_as=jnp.bfloat16):
    entries = jax.random.normal(stream_key, extent, jnp.float32) * width
    if len(shards) > 0:
        entries = block_levels(stream_key, extent, shards, -0.22, 0.18) * entries
    return jnp.clip(entries, min=-bound, max=bound).astype(held_as)


def setup_inputs(seed: int = 0) -> dict:
    splits = jax.random.split(jax.random.key(seed), 7)
    image_feats = bell_draw(splits[0], (BATCH, W), 1.0, 6.0, ((0, 32), (1, 16)))
    image_head = bell_draw(splits[1], (W, E), W ** -0.5, 0.15625, ((0, 16),))
    text_embed = bell_draw(splits[2], (BATCH, E), 1.0, 6.0, ((0, 32), (1, 16)))
    text_ids = jax.random.permutation(splits[3], BATCH).astype(jnp.int32)
    logit_scale = jnp.clip(jax.random.uniform(splits[4], (), jnp.float32, 4.0, 12.0), 4.0, 12.0)
    logit_bias = jnp.clip(jax.random.uniform(splits[5], (), jnp.float32, -2.0, 0.0), -2.0, 0.0)
    return dict(image_feats=image_feats, image_head=image_head, text_embed=text_embed, text_ids=text_ids, logit_scale=logit_scale, logit_bias=logit_bias)


def unit_rows(values):
    scale = lax.rsqrt(lax.optimization_barrier(jnp.sum(values * values, axis=1, keepdims=True)) + 1e-06)
    return (values * scale, scale)

def reference(image_feats, image_head, text_embed, text_ids, logit_scale, logit_bias):
    embed = jnp.dot(image_feats, image_head, preferred_element_type=jnp.float32)
    image_unit, image_scale = unit_rows(embed)
    text_unit, text_scale = unit_rows(text_embed.astype(jnp.float32))
    image_low = image_unit.astype(jnp.bfloat16)
    text_low = text_unit.astype(jnp.bfloat16)
    block = B_DEV

    def visit(carry, start):
        rows = lax.dynamic_slice_in_dim(image_low, start, block, 0)
        logits = logit_scale * jnp.dot(rows, text_low.T, preferred_element_type=jnp.float32) + logit_bias
        index = start + lax.broadcasted_iota(jnp.int32, (block, 1), 0)
        sign = jnp.where(index == text_ids[None, :].astype(jnp.int32), 1.0, -1.0).astype(logits.dtype)
        coef = (-sign * jax.nn.sigmoid(-sign * logits) * logit_scale).astype(jnp.bfloat16)
        grads = jnp.dot(coef, text_low, preferred_element_type=jnp.float32)
        carry = carry + jnp.dot(coef.T, rows, preferred_element_type=jnp.float32)
        return (carry, grads)
    starts = jnp.arange(N_DP, dtype=jnp.int32) * block
    text_acc, unit_blocks = lax.scan(visit, jnp.zeros((BATCH, E), jnp.float32), starts)
    unit_grad = unit_blocks.reshape(BATCH, E)
    embed_grad = (image_scale * (unit_grad - image_unit * lax.optimization_barrier(jnp.sum(image_unit * unit_grad, axis=1, keepdims=True)))).astype(jnp.bfloat16)
    text_grad = (text_scale * (text_acc - text_unit * lax.optimization_barrier(jnp.sum(text_unit * text_acc, axis=1, keepdims=True)))).astype(jnp.bfloat16)
    feature_grad = jnp.dot(embed_grad, image_head.T, preferred_element_type=jnp.float32).astype(jnp.bfloat16)
    head_grad = jnp.dot(image_feats.T, embed_grad, preferred_element_type=jnp.float32)
    return (feature_grad, head_grad, text_grad)
```

```python
import jax
import jax.numpy as jnp
from jax import lax
from jax.sharding import PartitionSpec as P

F32, BF16 = jnp.float32, jnp.bfloat16
X, ZH, CORE = 4, 2, 2
ZL, Y = 8, 4
PLANE = [[x * 4 + zh * 2 + c for x in range(X) for c in range(CORE)] for zh in range(ZH)]
LINE = [[z * Y + y for z in range(ZL)] for y in range(Y)]
RING = [[z * Y + y for y in range(Y)] for z in range(ZL)]
PAIR = [(i, i ^ 2) for i in range(16)]


def swap(value, axis, groups=None):
    return lax.all_to_all(value, axis, 0, 0, axis_index_groups=groups, tiled=True)


def spread(value, axis, groups, size):
    copies = jnp.broadcast_to(value[None], (size,) + value.shape)
    return swap(copies, axis, groups)


def on_device(image_feats, image_head, text_embed, text_ids, logit_scale, logit_bias):
    rows, width = image_feats.shape
    embed_width = image_head.shape[1]
    cycle = lax.axis_size("dp")
    group = lax.axis_size("fsdp")
    plane = X * CORE
    own = rows // plane
    held = -(-own // 8) * 8
    share = rows // group
    d = lax.axis_index("dp")
    f = lax.axis_index("fsdp")

    text_part = swap(text_embed.reshape(group, share, width), "fsdp")
    text_vals = text_part.transpose(1, 0, 2).reshape(share, embed_width).astype(F32)
    text_scale = lax.rsqrt(jnp.sum(text_vals * text_vals, axis=1, keepdims=True) + 1e-06)
    text_unit = text_vals * text_scale
    my_ids = lax.dynamic_slice_in_dim(text_ids, f * share, share, 0)
    marks = jnp.stack([my_ids // 128, my_ids % 128], axis=1).astype(BF16)
    marks = jnp.pad(marks, ((0, 0), (0, 126)))
    text_row = jnp.concatenate([text_unit.astype(BF16), marks], axis=1)
    line = spread(text_row, "dp", LINE, ZL).reshape(ZL * share, -1)
    texts = spread(line, "dp", RING, Y).reshape(cycle * share, -1)
    text_low = texts[:, :embed_width]
    ids = texts[:, embed_width].astype(jnp.int32) * 128 + texts[:, embed_width + 1].astype(jnp.int32)

    feats = jnp.pad(image_feats.reshape(plane, own, width), ((0, 0), (0, held - own), (0, 0)))
    feats = feats.reshape(plane * held, width)
    term = jnp.dot(feats, image_head, preferred_element_type=F32).astype(BF16)
    half = swap(term.reshape(plane, held, embed_width), "fsdp", PLANE)
    half = jnp.sum(half.astype(F32), axis=0).astype(BF16)
    embed = half.astype(F32) + lax.ppermute(half, "fsdp", PAIR).astype(F32)
    image_scale = lax.rsqrt(jnp.sum(embed * embed, axis=1, keepdims=True) + 1e-06)
    image_unit = embed * image_scale
    image_low = spread(image_unit.astype(BF16), "fsdp", PLANE, plane).reshape(plane * held, embed_width)

    partial_value = jnp.einsum("ie,je->ij", image_low, text_low, preferred_element_type=F32)
    logits = logit_scale * partial_value + logit_bias
    row = lax.broadcasted_iota(jnp.int32, (plane, held), 1)
    row_index = d * rows + lax.broadcasted_iota(jnp.int32, (plane, held), 0) * own + row
    row_index = jnp.where(row < own, row_index, -1).reshape(plane * held, 1)
    sign = jnp.where(row_index == ids[None, :], 1.0, -1.0).astype(F32)
    coef = (-sign * jax.nn.sigmoid(-sign * logits) * logit_scale).astype(BF16)
    unit_part = jnp.einsum("ij,je->ie", coef, text_low, preferred_element_type=F32).astype(BF16)
    text_acc = jnp.einsum("ij,ie->je", coef, image_low, preferred_element_type=F32).astype(BF16)

    back = swap(unit_part.reshape(plane, held, embed_width), "fsdp", PLANE)
    back = jnp.sum(back.astype(F32), axis=0).astype(BF16)
    unit_grad = back.astype(F32) + lax.ppermute(back, "fsdp", PAIR).astype(F32)
    image_dot = jnp.sum(image_unit * unit_grad, axis=1, keepdims=True)
    embed_grad = (image_scale * (unit_grad - image_unit * image_dot)).astype(BF16)
    grads = spread(embed_grad, "fsdp", PLANE, plane).reshape(plane * held, embed_width)
    lanes = embed_width // 128
    head_part = jnp.einsum("rw,re->we", feats, grads, preferred_element_type=F32).astype(BF16)
    head_part = head_part.reshape(width, lanes, 128).transpose(1, 0, 2).reshape(cycle, -1, 128)
    head_sum = jnp.sum(swap(head_part, "dp").astype(F32), axis=0).astype(BF16)
    head_all = spread(head_sum, "dp", None, cycle)
    head_grad = head_all.reshape(lanes, width, 128).transpose(1, 0, 2).reshape(width, embed_width).astype(F32)
    feature_grad = jnp.einsum("re,we->rw", grads, image_head, preferred_element_type=F32).astype(BF16)
    feature_grad = feature_grad.reshape(plane, held, width)[:, :own].reshape(rows, width)

    text_acc = swap(text_acc.reshape(Y, ZL * share, embed_width), "dp", RING)
    text_acc = jnp.sum(text_acc.astype(F32), axis=0).astype(BF16)
    text_acc = swap(text_acc.reshape(ZL, share, embed_width), "dp", LINE)
    text_acc = jnp.sum(text_acc.astype(F32), axis=0)
    text_dot = jnp.sum(text_unit * text_acc, axis=1, keepdims=True)
    text_rows = (text_scale * (text_acc - text_unit * text_dot)).astype(BF16)
    text_rows = text_rows.reshape(share, group, width).transpose(1, 0, 2)
    text_grad = swap(text_rows, "fsdp").reshape(rows, width)
    return (feature_grad, head_grad, text_grad)


def solution(mesh):
    placed = (P("dp", "fsdp"), P("fsdp", None), P("dp", "fsdp"), P("dp"), P(), P())
    return jax.shard_map(
        on_device,
        mesh=mesh,
        in_specs=placed,
        out_specs=(P("dp", "fsdp"), P("fsdp", None), P("dp", "fsdp")),
        check_vma=False,
    )
```

```python
import jax
import jax.numpy as jnp
from jax import lax
from jax.sharding import PartitionSpec as P

F32, BF16 = jnp.float32, jnp.bfloat16
ZL, Y, X, ZH, CORE = 8, 4, 4, 2, 2
PLANE = [[x * 4 + zh * 2 + c for x in range(X) for c in range(CORE)] for zh in range(ZH)]
PAIR = [(i, i ^ 2) for i in range(16)]


def moves(target):
    pairs = []
    for zl in range(ZL):
        for y in range(Y):
            for x in range(X):
                for zh in range(ZH):
                    for c in range(CORE):
                        a, b, e, g, h = target(zl, y, x, zh, c)
                        there = ((a * Y + b) * X + e) * 4 + g * 2 + h
                        pairs.append((((zl * Y + y) * X + x) * 4 + zh * 2 + c, there))
    return pairs


def along_z(by):
    def target(zl, y, x, zh, c):
        step = by if abs(by) < 4 or c == 0 else -by
        z = (zh * ZL + zl + step) % 16
        return z % ZL, y, x, z // ZL, c

    return moves(target)


def along_line(by):
    return moves(lambda zl, y, x, zh, c: ((zl + by) % ZL, y, x, zh, c))


def along_y(by):
    return moves(lambda zl, y, x, zh, c: (zl, (y + by) % Y, x, zh, c))


def along_plane(by):
    def target(zl, y, x, zh, c):
        k = (x * CORE + c + by) % (X * CORE)
        return zl, y, k // CORE, zh, k % CORE

    return moves(target)


def send(value, pairs):
    return lax.ppermute(value, ("dp", "fsdp"), pairs)


def swap(value, axis, groups=None):
    return lax.all_to_all(value, axis, 0, 0, axis_index_groups=groups, tiled=True)


def spread(value, axis, groups, size):
    copies = jnp.broadcast_to(value[None], (size,) + value.shape)
    return swap(copies, axis, groups)


Z_STEPS = (1, -1, 2, -2, 3, -3, 4)
Y_STEPS = (1, -1, 2)


def on_device(image_feats, image_head, text_embed, text_ids, logit_scale, logit_bias):
    rows, width = image_feats.shape
    embed_width = image_head.shape[1]
    cycle = lax.axis_size("dp")
    plane = X * CORE
    own = rows // plane
    held = -(-own // 8) * 8
    share = own // ZH
    piece = -(-share // 8) * 8
    d = lax.axis_index("dp")
    f = lax.axis_index("fsdp")
    zl, zh = d // Y, (f // CORE) % ZH
    k = (f // 4) * CORE + f % CORE

    parts = text_embed.reshape(X, 1, CORE, own, width)
    parts = jnp.broadcast_to(parts, (X, ZH, CORE, own, width)).reshape(X * ZH * CORE, own, width)
    text_part = swap(parts, "fsdp")
    text_vals = text_part.transpose(1, 0, 2).reshape(own, embed_width).astype(F32)
    text_scale = lax.rsqrt(jnp.sum(text_vals * text_vals, axis=1, keepdims=True) + 1e-06)
    text_unit = text_vals * text_scale
    my_ids = lax.dynamic_slice_in_dim(text_ids, k * own, own, 0).reshape(ZH, share)
    marks = jnp.concatenate([my_ids // 128, my_ids % 128], axis=1).astype(BF16)
    marks = jnp.pad(marks[:, None], ((0, 0), (0, piece - share - 1), (0, embed_width - 2 * share)))
    halves = jnp.concatenate([text_unit.astype(BF16).reshape(ZH, share, embed_width), marks], axis=1)
    first = zh == 0
    mine = jnp.where(first, halves[0], halves[1])
    other = jnp.where(first, halves[1], halves[0])
    unit_mine = jnp.where(first, text_unit[:share], text_unit[share:])
    scale_mine = jnp.where(first, text_scale[:share], text_scale[share:])

    blocks = [mine]
    core = f % CORE
    for by in Z_STEPS:
        step = jnp.where(core == 0, by, -by) if by == 4 else by
        there = (zh * ZL + zl + step + 16) % 16 // ZL
        blocks.append(send(jnp.where(there == zh, mine, other), along_z(by)))
    blocks = jnp.stack(blocks)
    line = blocks[:, :share].reshape(ZL * share, embed_width)
    line = jnp.concatenate([line, blocks[:, share]], axis=0)
    lines = [line] + [send(line, along_y(by)) for by in Y_STEPS]
    count = ZL * share
    texts = jnp.concatenate([part[:count] for part in lines], axis=0)
    notes = jnp.stack([part[count:, : 2 * share] for part in lines]).astype(jnp.int32)
    ids = (notes[:, :, :share] * 128 + notes[:, :, share:]).reshape(cycle * share)

    feats = jnp.pad(image_feats.reshape(plane, own, width), ((0, 0), (0, held - own), (0, 0)))
    feats = feats.reshape(plane * held, width)
    term = jnp.dot(feats, image_head, preferred_element_type=F32).astype(BF16)
    half = swap(term.reshape(plane, held, embed_width), "fsdp", PLANE)
    half = jnp.sum(half.astype(F32), axis=0).astype(BF16)
    embed = half.astype(F32) + lax.ppermute(half, "fsdp", PAIR).astype(F32)
    image_scale = lax.rsqrt(jnp.sum(embed * embed, axis=1, keepdims=True) + 1e-06)
    image_unit = embed * image_scale
    image_low = spread(image_unit.astype(BF16), "fsdp", PLANE, plane).reshape(plane * held, embed_width)

    partial_value = jnp.einsum("ie,je->ij", image_low, texts, preferred_element_type=F32)
    logits = logit_scale * partial_value + logit_bias
    row = lax.broadcasted_iota(jnp.int32, (plane, held), 1)
    row_index = d * rows + lax.broadcasted_iota(jnp.int32, (plane, held), 0) * own + row
    row_index = jnp.where(row < own, row_index, -1).reshape(plane * held, 1)
    sign = jnp.where(row_index == ids[None, :], 1.0, -1.0).astype(F32)
    coef = (-sign * jax.nn.sigmoid(-sign * logits) * logit_scale).astype(BF16)
    unit_part = jnp.einsum("ij,je->ie", coef, texts, preferred_element_type=F32).astype(BF16)
    text_acc = jnp.einsum("ij,ie->je", coef, image_low, preferred_element_type=F32).astype(BF16)

    back = swap(unit_part.reshape(plane, held, embed_width), "fsdp", PLANE)
    back = jnp.sum(back.astype(F32), axis=0).astype(BF16)
    unit_grad = back.astype(F32) + lax.ppermute(back, "fsdp", PAIR).astype(F32)
    image_dot = jnp.sum(image_unit * unit_grad, axis=1, keepdims=True)
    embed_grad = (image_scale * (unit_grad - image_unit * image_dot)).astype(BF16)
    grads = spread(embed_grad, "fsdp", PLANE, plane).reshape(plane * held, embed_width)
    lanes = embed_width // 128
    head_part = jnp.einsum("rw,re->we", feats, grads, preferred_element_type=F32).astype(BF16)
    head_part = head_part.reshape(width, lanes, 128).transpose(1, 0, 2).reshape(cycle, -1, 128)
    head_sum = jnp.sum(swap(head_part, "dp").astype(F32), axis=0).astype(BF16)
    head_all = spread(head_sum, "dp", None, cycle)
    head_grad = head_all.reshape(lanes, width, 128).transpose(1, 0, 2).reshape(width, embed_width).astype(F32)
    feature_grad = jnp.einsum("re,we->rw", grads, image_head, preferred_element_type=F32).astype(BF16)
    feature_grad = feature_grad.reshape(plane, held, width)[:, :own].reshape(rows, width)

    text_acc = text_acc.reshape(Y, count, embed_width)
    total = text_acc[0].astype(F32)
    for slot, by in enumerate(Y_STEPS):
        total = total + send(text_acc[slot + 1], along_y(-by)).astype(F32)
    total = total.astype(BF16).reshape(ZL, share, embed_width)
    text_grads = total[0].astype(F32)
    for slot, by in enumerate(Z_STEPS):
        text_grads = text_grads + send(total[slot + 1], along_line(-by)).astype(F32)
    text_dot = jnp.sum(unit_mine * text_grads, axis=1, keepdims=True)
    text_rows = (scale_mine * (text_grads - unit_mine * text_dot)).astype(BF16)
    text_rows = text_rows.reshape(share, X, ZH, CORE, width).transpose(2, 1, 3, 0, 4)
    near = jnp.where(first, text_rows[0], text_rows[1])
    far = jnp.where(first, text_rows[1], text_rows[0])
    came = lax.ppermute(far, "fsdp", PAIR)
    both = jnp.where(first, jnp.stack([near, came], axis=2), jnp.stack([came, near], axis=2))
    both = both.reshape(plane, own, width)
    turned = lax.dynamic_slice_in_dim(jnp.concatenate([both, both], axis=0), k, plane, 0)
    got = [turned[0]] + [send(turned[by], along_plane(by)) for by in range(1, plane)]
    got = jnp.stack(got[::-1] * 2)
    text_grad = lax.dynamic_slice_in_dim(got, plane - 1 - k, plane, 0).reshape(rows, width)
    return (feature_grad, head_grad, text_grad)


def solution(mesh):
    placed = (P("dp", "fsdp"), P("fsdp", None), P("dp", "fsdp"), P("dp"), P(), P())
    return jax.shard_map(
        on_device,
        mesh=mesh,
        in_specs=placed,
        out_specs=(P("dp", "fsdp"), P("fsdp", None), P("dp", "fsdp")),
        check_vma=False,
    )
```

```python
import jax
import jax.numpy as jnp
from jax import lax
from jax.sharding import PartitionSpec as P

F32, BF16 = jnp.float32, jnp.bfloat16
X, ZH, CORE = 4, 2, 2
ZL, Y = 8, 4
PLANE = [[x * 4 + zh * 2 + c for x in range(X) for c in range(CORE)] for zh in range(ZH)]
LINE = [[z * Y + y for z in range(ZL)] for y in range(Y)]
RING = [[z * Y + y for y in range(Y)] for z in range(ZL)]
PAIR = [(i, i ^ 2) for i in range(16)]


def swap(value, axis, groups=None):
    return lax.all_to_all(value, axis, 0, 0, axis_index_groups=groups, tiled=True)


def spread(value, axis, groups, size):
    copies = jnp.broadcast_to(value[None], (size,) + value.shape)
    return swap(copies, axis, groups)


def on_device(image_feats, image_head, text_embed, text_ids, logit_scale, logit_bias):
    rows, width = image_feats.shape
    embed_width = image_head.shape[1]
    cycle = lax.axis_size("dp")
    group = lax.axis_size("fsdp")
    plane = X * CORE
    own = rows // plane
    held = -(-own // 8) * 8
    share = rows // group
    d = lax.axis_index("dp")
    f = lax.axis_index("fsdp")

    text_part = swap(text_embed.reshape(group, share, width), "fsdp")
    text_vals = text_part.transpose(1, 0, 2).reshape(share, embed_width).astype(F32)
    text_scale = lax.rsqrt(jnp.sum(text_vals * text_vals, axis=1, keepdims=True) + 1e-06)
    text_unit = text_vals * text_scale
    my_ids = lax.dynamic_slice_in_dim(text_ids, f * share, share, 0)
    marks = jnp.concatenate([my_ids // 128, my_ids % 128]).astype(BF16)
    piece = -(-share // 8) * 8
    marks = jnp.pad(marks[None], ((0, piece - share - 1), (0, embed_width - 2 * share)))
    block = jnp.concatenate([text_unit.astype(BF16), marks], axis=0)
    blocks = lax.all_gather(block, "dp", axis_index_groups=LINE)
    count = ZL * share
    line = jnp.concatenate([blocks[:, :share].reshape(count, embed_width), blocks[:, share]], axis=0)
    lines = lax.all_gather(line, "dp", axis_index_groups=RING)
    text_low = lines[:, :count].reshape(cycle * share, embed_width)
    notes = lines[:, count:, : 2 * share].astype(jnp.int32)
    ids = (notes[:, :, :share] * 128 + notes[:, :, share:]).reshape(cycle * share)

    feats = jnp.pad(image_feats.reshape(plane, own, width), ((0, 0), (0, held - own), (0, 0)))
    feats = feats.reshape(plane * held, width)
    term = jnp.dot(feats, image_head, preferred_element_type=F32).astype(BF16)
    half = swap(term.reshape(plane, held, embed_width), "fsdp", PLANE)
    half = jnp.sum(half.astype(F32), axis=0).astype(BF16)
    embed = half.astype(F32) + lax.ppermute(half, "fsdp", PAIR).astype(F32)
    image_scale = lax.rsqrt(jnp.sum(embed * embed, axis=1, keepdims=True) + 1e-06)
    image_unit = embed * image_scale
    image_low = spread(image_unit.astype(BF16), "fsdp", PLANE, plane).reshape(plane * held, embed_width)

    partial_value = jnp.einsum("ie,je->ij", image_low, text_low, preferred_element_type=F32)
    logits = logit_scale * partial_value + logit_bias
    row = lax.broadcasted_iota(jnp.int32, (plane, held), 1)
    row_index = d * rows + lax.broadcasted_iota(jnp.int32, (plane, held), 0) * own + row
    row_index = jnp.where(row < own, row_index, -1).reshape(plane * held, 1)
    sign = jnp.where(row_index == ids[None, :], 1.0, -1.0).astype(F32)
    coef = (-sign * jax.nn.sigmoid(-sign * logits) * logit_scale).astype(BF16)
    unit_part = jnp.einsum("ij,je->ie", coef, text_low, preferred_element_type=F32).astype(BF16)
    text_acc = jnp.einsum("ij,ie->je", coef, image_low, preferred_element_type=F32).astype(BF16)

    back = swap(unit_part.reshape(plane, held, embed_width), "fsdp", PLANE)
    back = jnp.sum(back.astype(F32), axis=0).astype(BF16)
    unit_grad = back.astype(F32) + lax.ppermute(back, "fsdp", PAIR).astype(F32)
    image_dot = jnp.sum(image_unit * unit_grad, axis=1, keepdims=True)
    embed_grad = (image_scale * (unit_grad - image_unit * image_dot)).astype(BF16)
    grads = spread(embed_grad, "fsdp", PLANE, plane).reshape(plane * held, embed_width)
    lanes = embed_width // 128
    head_part = jnp.einsum("rw,re->we", feats, grads, preferred_element_type=F32).astype(BF16)
    head_part = head_part.reshape(width, lanes, 128).transpose(1, 0, 2).reshape(cycle, -1, 128)
    head_sum = jnp.sum(swap(head_part, "dp").astype(F32), axis=0).astype(BF16)
    head_all = spread(head_sum, "dp", None, cycle)
    head_grad = head_all.reshape(lanes, width, 128).transpose(1, 0, 2).reshape(width, embed_width).astype(F32)
    feature_grad = jnp.einsum("re,we->rw", grads, image_head, preferred_element_type=F32).astype(BF16)
    feature_grad = feature_grad.reshape(plane, held, width)[:, :own].reshape(rows, width)

    text_acc = lax.psum_scatter(text_acc.reshape(Y, count, embed_width), "dp", axis_index_groups=RING)
    text_acc = lax.psum_scatter(text_acc.reshape(ZL, share, embed_width), "dp", axis_index_groups=LINE)
    text_acc = text_acc.astype(F32)
    text_dot = jnp.sum(text_unit * text_acc, axis=1, keepdims=True)
    text_rows = (text_scale * (text_acc - text_unit * text_dot)).astype(BF16)
    text_rows = text_rows.reshape(share, group, width).transpose(1, 0, 2)
    text_grad = swap(text_rows, "fsdp").reshape(rows, width)
    return (feature_grad, head_grad, text_grad)


def solution(mesh):
    placed = (P("dp", "fsdp"), P("fsdp", None), P("dp", "fsdp"), P("dp"), P(), P())
    return jax.shard_map(
        on_device,
        mesh=mesh,
        in_specs=placed,
        out_specs=(P("dp", "fsdp"), P("fsdp", None), P("dp", "fsdp")),
        check_vma=False,
    )
```

```python
import jax
import jax.numpy as jnp
from jax import lax
from jax.sharding import PartitionSpec as P

F32, BF16 = jnp.float32, jnp.bfloat16
X, ZH, CORE = 4, 2, 2
ZL, Y = 8, 4
PLANE = [[x * 4 + zh * 2 + c for x in range(X) for c in range(CORE)] for zh in range(ZH)]
LINE = [[z * Y + y for z in range(ZL)] for y in range(Y)]
RING = [[z * Y + y for y in range(Y)] for z in range(ZL)]
PAIR = [(i, i ^ 2) for i in range(16)]
QUAD = [[(q * 4 + i) * Y + y for i in range(4)] for q in range(ZL // 4) for y in range(Y)]
ACROSS = [(i, i ^ (4 * Y)) for i in range(ZL * Y)]


def swap(value, axis, groups=None):
    return lax.all_to_all(value, axis, 0, 0, axis_index_groups=groups, tiled=True)


def spread(value, axis, groups, size):
    copies = jnp.broadcast_to(value[None], (size,) + value.shape)
    return swap(copies, axis, groups)


def on_device(image_feats, image_head, text_embed, text_ids, logit_scale, logit_bias):
    rows, width = image_feats.shape
    embed_width = image_head.shape[1]
    cycle = lax.axis_size("dp")
    group = lax.axis_size("fsdp")
    plane = X * CORE
    own = rows // plane
    held = -(-own // 8) * 8
    share = rows // group
    d = lax.axis_index("dp")
    f = lax.axis_index("fsdp")

    text_part = swap(text_embed.reshape(group, share, width), "fsdp")
    text_vals = text_part.transpose(1, 0, 2).reshape(share, embed_width).astype(F32)
    text_scale = lax.rsqrt(jnp.sum(text_vals * text_vals, axis=1, keepdims=True) + 1e-06)
    text_unit = text_vals * text_scale
    my_ids = lax.dynamic_slice_in_dim(text_ids, f * share, share, 0)
    marks = jnp.concatenate([my_ids // 128, my_ids % 128]).astype(BF16)
    piece = -(-share // 8) * 8
    marks = jnp.pad(marks[None], ((0, piece - share - 1), (0, embed_width - 2 * share)))
    block = jnp.concatenate([text_unit.astype(BF16), marks], axis=0)
    blocks = spread(block, "dp", QUAD, 4).reshape(4, piece, embed_width)
    count = 4 * share
    quad = jnp.concatenate([blocks[:, :share].reshape(count, embed_width), blocks[:, share]], axis=0)
    quad = jnp.pad(quad, ((0, 4), (0, 0)))

    feats = jnp.pad(image_feats.reshape(plane, own, width), ((0, 0), (0, held - own), (0, 0)))
    feats = feats.reshape(plane * held, width)
    term = jnp.dot(feats, image_head, preferred_element_type=F32).astype(BF16)
    term, quad = lax.optimization_barrier((term, quad))
    crossed = lax.ppermute(quad, "dp", ACROSS)
    half = swap(term.reshape(plane, held, embed_width), "fsdp", PLANE)
    half = jnp.sum(half.astype(F32), axis=0).astype(BF16)
    line = jnp.stack([quad, crossed])
    half, line = lax.optimization_barrier((half, line))

    lines = lax.all_gather(line, "dp", axis_index_groups=RING)
    embed = half.astype(F32) + lax.ppermute(half, "fsdp", PAIR).astype(F32)
    image_scale = lax.rsqrt(jnp.sum(embed * embed, axis=1, keepdims=True) + 1e-06)
    image_unit = embed * image_scale
    image_low = spread(image_unit.astype(BF16), "fsdp", PLANE, plane).reshape(plane * held, embed_width)
    text_low = lines[:, :, :count].reshape(cycle * share, embed_width)
    notes = lines[:, :, count : count + 4, : 2 * share].astype(jnp.int32)
    ids = (notes[..., :share] * 128 + notes[..., share:]).reshape(cycle * share)

    partial_value = jnp.einsum("ie,je->ij", image_low, text_low, preferred_element_type=F32)
    logits = logit_scale * partial_value + logit_bias
    row = lax.broadcasted_iota(jnp.int32, (plane, held), 1)
    row_index = d * rows + lax.broadcasted_iota(jnp.int32, (plane, held), 0) * own + row
    row_index = jnp.where(row < own, row_index, -1).reshape(plane * held, 1)
    sign = jnp.where(row_index == ids[None, :], 1.0, -1.0).astype(F32)
    coef = (-sign * jax.nn.sigmoid(-sign * logits) * logit_scale).astype(BF16)
    unit_part = jnp.einsum("ij,je->ie", coef, text_low, preferred_element_type=F32).astype(BF16)
    text_acc = jnp.einsum("ij,ie->je", coef, image_low, preferred_element_type=F32).astype(BF16)

    unit_part, text_acc = lax.optimization_barrier((unit_part, text_acc))

    text_acc = lax.psum_scatter(text_acc.reshape(Y, ZL * share, embed_width), "dp", axis_index_groups=RING)
    back = swap(unit_part.reshape(plane, held, embed_width), "fsdp", PLANE)
    back = jnp.sum(back.astype(F32), axis=0).astype(BF16)
    unit_grad = back.astype(F32) + lax.ppermute(back, "fsdp", PAIR).astype(F32)
    image_dot = jnp.sum(image_unit * unit_grad, axis=1, keepdims=True)
    embed_grad = (image_scale * (unit_grad - image_unit * image_dot)).astype(BF16)
    text_acc = text_acc.reshape(2, 4, share, embed_width)
    text_acc = jnp.where(d // Y < 4, text_acc, text_acc[::-1]).reshape(ZL, share, embed_width)
    embed_grad, text_acc = lax.optimization_barrier((embed_grad, text_acc))
    text_acc = lax.psum_scatter(text_acc, "dp", axis_index_groups=LINE)
    grads = spread(embed_grad, "fsdp", PLANE, plane).reshape(plane * held, embed_width)
    head_part = jnp.einsum("rw,re->we", feats, grads, preferred_element_type=F32).astype(BF16)
    head_sum = jnp.sum(swap(head_part.reshape(Y, width // Y, embed_width), "dp", RING).astype(F32), axis=0)
    head_sum = head_sum.astype(BF16).reshape(width // Y, ZL, embed_width // ZL).transpose(1, 0, 2)
    head_sum = jnp.sum(swap(head_sum, "dp", LINE).astype(F32), axis=0).astype(BF16)
    head_all = spread(head_sum, "dp", LINE, ZL).transpose(1, 0, 2).reshape(width // Y, embed_width)
    head_all = spread(head_all, "dp", RING, Y).reshape(width, embed_width)
    head_all, text_acc = lax.optimization_barrier((head_all, text_acc))
    head_grad = head_all.astype(F32)
    feature_grad = jnp.einsum("re,we->rw", grads, image_head, preferred_element_type=F32).astype(BF16)
    feature_grad = feature_grad.reshape(plane, held, width)[:, :own].reshape(rows, width)

    text_acc = text_acc.astype(F32)
    text_dot = jnp.sum(text_unit * text_acc, axis=1, keepdims=True)
    text_rows = (text_scale * (text_acc - text_unit * text_dot)).astype(BF16)
    text_rows = text_rows.reshape(share, group, width).transpose(1, 0, 2)
    text_grad = swap(text_rows, "fsdp").reshape(rows, width)
    return (feature_grad, head_grad, text_grad)


def solution(mesh):
    placed = (P("dp", "fsdp"), P("fsdp", None), P("dp", "fsdp"), P("dp"), P(), P())
    return jax.shard_map(
        on_device,
        mesh=mesh,
        in_specs=placed,
        out_specs=(P("dp", "fsdp"), P("fsdp", None), P("dp", "fsdp")),
        check_vma=False,
    )
```

```python
import jax
import jax.numpy as jnp
from jax import lax
from jax.sharding import PartitionSpec as P

F32, BF16 = jnp.float32, jnp.bfloat16
X, ZH, CORE = 4, 2, 2
ZL, Y = 8, 4
PLANE = [[x * 4 + zh * 2 + c for x in range(X) for c in range(CORE)] for zh in range(ZH)]
FOLD = (0, 2, 4, 6, 7, 5, 3, 1)
LINE = [[z * Y + y for z in FOLD] for y in range(Y)]
RING = [[z * Y + y for y in range(Y)] for z in range(ZL)]
PAIR = [(i, i ^ 2) for i in range(16)]
QUAD = [[(q * 4 + i) * Y + y for i in range(4)] for q in range(ZL // 4) for y in range(Y)]
SLAB = [[(q * 4 + i) * Y + y for y in range(Y) for i in range(4)] for q in range(ZL // 4)]
ACROSS = [(i, i ^ (4 * Y)) for i in range(ZL * Y)]


def swap(value, axis, groups=None):
    return lax.all_to_all(value, axis, 0, 0, axis_index_groups=groups, tiled=True)


def spread(value, axis, groups, size):
    copies = jnp.broadcast_to(value[None], (size,) + value.shape)
    return swap(copies, axis, groups)


def on_device(image_feats, image_head, text_embed, text_ids, logit_scale, logit_bias):
    rows, width = image_feats.shape
    embed_width = image_head.shape[1]
    cycle = lax.axis_size("dp")
    group = lax.axis_size("fsdp")
    plane = X * CORE
    own = rows // plane
    held = -(-own // 8) * 8
    share = rows // group
    d = lax.axis_index("dp")
    f = lax.axis_index("fsdp")

    text_part = swap(text_embed.reshape(group, share, width), "fsdp")
    text_vals = text_part.transpose(1, 0, 2).reshape(share, embed_width).astype(F32)
    text_scale = lax.rsqrt(jnp.sum(text_vals * text_vals, axis=1, keepdims=True) + 1e-06)
    text_unit = text_vals * text_scale
    my_ids = lax.dynamic_slice_in_dim(text_ids, f * share, share, 0)
    marks = jnp.concatenate([my_ids // 128, my_ids % 128]).astype(BF16)
    piece = -(-share // 8) * 8
    marks = jnp.pad(marks[None], ((0, piece - share - 1), (0, embed_width - 2 * share)))
    block = jnp.concatenate([text_unit.astype(BF16), marks], axis=0)
    blocks = spread(block, "dp", QUAD, 4).reshape(4, piece, embed_width)
    count = 4 * share
    quad = jnp.concatenate([blocks[:, :share].reshape(count, embed_width), blocks[:, share]], axis=0)
    quad = jnp.pad(quad, ((0, 12), (0, 0)))

    feats = jnp.pad(image_feats.reshape(plane, own, width), ((0, 0), (0, held - own), (0, 0)))
    feats = feats.reshape(plane * held, width)
    term = jnp.dot(feats, image_head, preferred_element_type=F32).astype(BF16)
    term, quad = lax.optimization_barrier((term, quad))
    near = lax.all_gather(quad, "dp", axis_index_groups=RING)
    crossed = lax.ppermute(quad, "dp", ACROSS)
    half = swap(term.reshape(plane, held, embed_width), "fsdp", PLANE)
    half = jnp.sum(half.astype(F32), axis=0).astype(BF16)
    half, crossed = lax.optimization_barrier((half, crossed))

    far = lax.all_gather(crossed, "dp", axis_index_groups=RING)
    embed = half.astype(F32) + lax.ppermute(half, "fsdp", PAIR).astype(F32)
    image_scale = lax.rsqrt(jnp.sum(embed * embed, axis=1, keepdims=True) + 1e-06)
    image_unit = embed * image_scale
    image_low = spread(image_unit.astype(BF16), "fsdp", PLANE, plane).reshape(plane * held, embed_width)
    lines = (near, far)
    text_low = jnp.concatenate([part[:, :count] for part in lines]).reshape(cycle * share, embed_width)
    notes = jnp.concatenate([part[:, count : count + 4, : 2 * share] for part in lines]).astype(jnp.int32)
    ids = (notes[..., :share] * 128 + notes[..., share:]).reshape(cycle * share)

    partial_value = jnp.einsum("ie,je->ij", image_low, text_low, preferred_element_type=F32)
    logits = logit_scale * partial_value + logit_bias
    row = lax.broadcasted_iota(jnp.int32, (plane, held), 1)
    row_index = d * rows + lax.broadcasted_iota(jnp.int32, (plane, held), 0) * own + row
    row_index = jnp.where(row < own, row_index, -1).reshape(plane * held, 1)
    sign = jnp.where(row_index == ids[None, :], 1.0, -1.0).astype(F32)
    coef = (-sign * jax.nn.sigmoid(-sign * logits) * logit_scale).astype(BF16)
    unit_part = jnp.einsum("ij,je->ie", coef, text_low, preferred_element_type=F32).astype(BF16)
    text_acc = jnp.einsum("ij,ie->je", coef, image_low, preferred_element_type=F32).astype(BF16)

    unit_part, text_acc = lax.optimization_barrier((unit_part, text_acc))

    text_acc = text_acc.reshape(2, Y, 4 * share, embed_width).transpose(1, 0, 2, 3)
    text_acc = lax.psum_scatter(text_acc.reshape(Y, ZL * share, embed_width), "dp", axis_index_groups=RING)
    back = swap(unit_part.reshape(plane, held, embed_width), "fsdp", PLANE)
    back = jnp.sum(back.astype(F32), axis=0).astype(BF16)
    unit_grad = back.astype(F32) + lax.ppermute(back, "fsdp", PAIR).astype(F32)
    image_dot = jnp.sum(image_unit * unit_grad, axis=1, keepdims=True)
    embed_grad = (image_scale * (unit_grad - image_unit * image_dot)).astype(BF16)
    text_acc = text_acc.reshape(2, 4, share, embed_width)
    text_acc = jnp.where(d // Y < 4, text_acc, text_acc[::-1]).reshape(ZL, share, embed_width)
    text_acc = jnp.stack([text_acc[z] for z in FOLD])
    embed_grad, text_acc = lax.optimization_barrier((embed_grad, text_acc))
    text_acc = lax.psum_scatter(text_acc, "dp", axis_index_groups=LINE)
    grads = spread(embed_grad, "fsdp", PLANE, plane).reshape(plane * held, embed_width)
    head_part = jnp.einsum("rw,re->we", feats, grads, preferred_element_type=F32).astype(BF16)
    head_part = head_part.reshape(Y, width // Y, 4, embed_width // 4).transpose(0, 2, 1, 3)
    head_part = head_part.reshape(4 * Y, width // Y, embed_width // 4)
    head_sum = jnp.sum(swap(head_part, "dp", SLAB).astype(F32), axis=0)
    head_sum = lax.reduce_precision(head_sum, 8, 7)
    head_sum = head_sum + lax.ppermute(head_sum.astype(BF16), "dp", ACROSS).astype(F32)
    head_sum, text_acc = lax.optimization_barrier((head_sum.astype(BF16), text_acc))
    head_all = spread(head_sum, "dp", SLAB, 4 * Y).reshape(Y, 4, width // Y, embed_width // 4)
    head_all = head_all.transpose(0, 2, 1, 3).reshape(width, embed_width)
    head_grad = head_all.astype(F32)
    feature_grad = jnp.einsum("re,we->rw", grads, image_head, preferred_element_type=F32).astype(BF16)
    feature_grad = feature_grad.reshape(plane, held, width)[:, :own].reshape(rows, width)

    text_acc = text_acc.astype(F32)
    text_dot = jnp.sum(text_unit * text_acc, axis=1, keepdims=True)
    text_rows = (text_scale * (text_acc - text_unit * text_dot)).astype(BF16)
    text_rows = text_rows.reshape(share, group, width).transpose(1, 0, 2)
    text_grad = swap(text_rows, "fsdp").reshape(rows, width)
    return (feature_grad, head_grad, text_grad)


def solution(mesh):
    placed = (P("dp", "fsdp"), P("fsdp", None), P("dp", "fsdp"), P("dp"), P(), P())
    return jax.shard_map(
        on_device,
        mesh=mesh,
        in_specs=placed,
        out_specs=(P("dp", "fsdp"), P("fsdp", None), P("dp", "fsdp")),
        check_vma=False,
    )
```

```python
import jax
import jax.numpy as jnp
from jax import lax
from jax.sharding import PartitionSpec as P

F32, BF16 = jnp.float32, jnp.bfloat16
X, ZH, CORE = 4, 2, 2
ZL, Y = 8, 4
PLANE = [[x * 4 + zh * 2 + c for x in range(X) for c in range(CORE)] for zh in range(ZH)]
RING = [[z * Y + y for y in range(Y)] for z in range(ZL)]
PAIR = [(i, i ^ 2) for i in range(16)]
QUAD = [[(q * 4 + i) * Y + y for i in range(4)] for q in range(ZL // 4) for y in range(Y)]
SLAB = [[(q * 4 + i) * Y + y for y in range(Y) for i in range(4)] for q in range(ZL // 4)]
ACROSS = [(i, i ^ (4 * Y)) for i in range(ZL * Y)]


def place(z, y, x, c):
    return ((z % ZL * Y + y) * X + x) * 4 + z % 16 // ZL * 2 + c


def mirror(z):
    edge = z // 4 * 4 if z % 4 < 2 else z // 4 * 4 + 4
    return (2 * edge - 1 - z) % 16


COLUMNS = [(y, x, c) for y in range(Y) for x in range(X) for c in range(CORE)]
MIRROR = [(place(z, *at), place(mirror(z), *at)) for z in range(16) for at in COLUMNS]
FOLD = (0, 2, 4, 6, 7, 5, 3, 1)
LINE = [[place(z0 + p, *at) for p in FOLD] for z0 in (14, 6) for at in COLUMNS]
LINE_ZL = [(6 + p) % ZL for p in FOLD]


def swap(value, axis, groups=None):
    return lax.all_to_all(value, axis, 0, 0, axis_index_groups=groups, tiled=True)


def spread(value, axis, groups, size):
    copies = jnp.broadcast_to(value[None], (size,) + value.shape)
    return swap(copies, axis, groups)


def on_device(image_feats, image_head, text_embed, text_ids, logit_scale, logit_bias):
    rows, width = image_feats.shape
    embed_width = image_head.shape[1]
    cycle = lax.axis_size("dp")
    group = lax.axis_size("fsdp")
    plane = X * CORE
    own = rows // plane
    held = -(-own // 8) * 8
    share = own // ZH
    d = lax.axis_index("dp")
    f = lax.axis_index("fsdp")

    zl, zh = d // Y, f // CORE % ZH
    k = f // 4 * CORE + f % CORE
    z = zh * ZL + zl
    second = (z >= 6) & (z < 14)
    parts = jnp.broadcast_to(text_embed.reshape(X, 1, CORE, own, width), (X, ZH, CORE, own, width))
    text_part = swap(parts.reshape(group, own, width), "fsdp")
    text_vals = text_part.transpose(1, 0, 2).reshape(own, embed_width).astype(F32)
    text_scale = lax.rsqrt(jnp.sum(text_vals * text_vals, axis=1, keepdims=True) + 1e-06)
    text_unit = text_vals * text_scale
    my_ids = lax.dynamic_slice_in_dim(text_ids, k * own, own, 0).reshape(ZH, share)
    marks = jnp.concatenate([my_ids // 128, my_ids % 128], axis=1).astype(BF16)
    piece = -(-share // 8) * 8
    marks = jnp.pad(marks[:, None], ((0, 0), (0, piece - share - 1), (0, embed_width - 2 * share)))
    halves = jnp.concatenate([text_unit.astype(BF16).reshape(ZH, share, embed_width), marks], axis=1)
    text_unit = jnp.where(second, text_unit[share:], text_unit[:share])
    text_scale = jnp.where(second, text_scale[share:], text_scale[:share])
    there = z // 4 * 4 + jnp.arange(4)
    there = ((there >= 6) & (there < 14))[:, None, None]
    blocks = swap(jnp.where(there, halves[1], halves[0]), "dp", QUAD)
    count = 4 * share
    quad = jnp.concatenate([blocks[:, :share].reshape(count, embed_width), blocks[:, share]], axis=0)
    quad = jnp.pad(quad, ((0, 12), (0, 0)))

    feats = jnp.pad(image_feats.reshape(plane, own, width), ((0, 0), (0, held - own), (0, 0)))
    feats = feats.reshape(plane * held, width)
    term = jnp.dot(feats, image_head, preferred_element_type=F32).astype(BF16)
    term, quad = lax.optimization_barrier((term, quad))
    near = lax.all_gather(quad, "dp", axis_index_groups=RING)
    crossed = lax.ppermute(quad, ("dp", "fsdp"), MIRROR)
    half = swap(term.reshape(plane, held, embed_width), "fsdp", PLANE)
    half = jnp.sum(half.astype(F32), axis=0).astype(BF16)

    far = lax.all_gather(crossed, "dp", axis_index_groups=RING)
    embed = half.astype(F32) + lax.ppermute(half, "fsdp", PAIR).astype(F32)
    image_scale = lax.rsqrt(jnp.sum(embed * embed, axis=1, keepdims=True) + 1e-06)
    image_unit = embed * image_scale
    image_low = spread(image_unit.astype(BF16), "fsdp", PLANE, plane).reshape(plane * held, embed_width)
    lines = (near, far)
    text_low = jnp.concatenate([part[:, :count] for part in lines]).reshape(cycle * share, embed_width)
    notes = jnp.concatenate([part[:, count : count + 4, : 2 * share] for part in lines]).astype(jnp.int32)
    ids = (notes[..., :share] * 128 + notes[..., share:]).reshape(cycle * share)

    partial_value = jnp.einsum("ie,je->ij", image_low, text_low, preferred_element_type=F32)
    logits = logit_scale * partial_value + logit_bias
    row = lax.broadcasted_iota(jnp.int32, (plane, held), 1)
    row_index = d * rows + lax.broadcasted_iota(jnp.int32, (plane, held), 0) * own + row
    row_index = jnp.where(row < own, row_index, -1).reshape(plane * held, 1)
    sign = jnp.where(row_index == ids[None, :], 1.0, -1.0).astype(F32)
    coef = (-sign * jax.nn.sigmoid(-sign * logits) * logit_scale).astype(BF16)
    unit_part = jnp.einsum("ij,je->ie", coef, text_low, preferred_element_type=F32).astype(BF16)
    text_acc = jnp.einsum("ij,ie->je", coef, image_low, preferred_element_type=F32).astype(BF16)


    text_acc = text_acc.reshape(2, Y, 4 * share, embed_width).transpose(1, 0, 2, 3)
    text_acc = lax.psum_scatter(text_acc.reshape(Y, ZL * share, embed_width), "dp", axis_index_groups=RING)
    back = swap(unit_part.reshape(plane, held, embed_width), "fsdp", PLANE)
    back = jnp.sum(back.astype(F32), axis=0).astype(BF16)
    unit_grad = back.astype(F32) + lax.ppermute(back, "fsdp", PAIR).astype(F32)
    image_dot = jnp.sum(image_unit * unit_grad, axis=1, keepdims=True)
    embed_grad = (image_scale * (unit_grad - image_unit * image_dot)).astype(BF16)
    text_acc = text_acc.reshape(2, 4, share, embed_width)
    text_acc = jnp.where(zl < 4, text_acc, text_acc[::-1]).reshape(ZL, share, embed_width)
    text_acc = jnp.stack([text_acc[at] for at in LINE_ZL])
    embed_grad, text_acc = lax.optimization_barrier((embed_grad, text_acc))
    text_acc = lax.psum_scatter(text_acc, ("dp", "fsdp"), axis_index_groups=LINE)
    grads = spread(embed_grad, "fsdp", PLANE, plane).reshape(plane * held, embed_width)
    head_part = jnp.einsum("rw,re->we", feats, grads, preferred_element_type=F32).astype(BF16)
    head_part = head_part.reshape(Y, width // Y, 4, embed_width // 4).transpose(0, 2, 1, 3)
    head_part = head_part.reshape(4 * Y, width // Y, embed_width // 4)
    head_sum = jnp.sum(swap(head_part, "dp", SLAB).astype(F32), axis=0)
    head_sum, text_acc = lax.optimization_barrier((head_sum, text_acc))
    head_sum = lax.reduce_precision(head_sum, 8, 7)
    head_sum = head_sum + lax.ppermute(head_sum.astype(BF16), "dp", ACROSS).astype(F32)
    head_all = spread(head_sum.astype(BF16), "dp", SLAB, 4 * Y).reshape(Y, 4, width // Y, embed_width // 4)
    head_all = head_all.transpose(0, 2, 1, 3).reshape(width, embed_width)
    head_grad = head_all.astype(F32)
    feature_grad = jnp.einsum("re,we->rw", grads, image_head, preferred_element_type=F32).astype(BF16)
    feature_grad = feature_grad.reshape(plane, held, width)[:, :own].reshape(rows, width)

    text_acc = text_acc.astype(F32)
    text_dot = jnp.sum(text_unit * text_acc, axis=1, keepdims=True)
    text_rows = (text_scale * (text_acc - text_unit * text_dot)).astype(BF16)
    text_rows = text_rows.reshape(share, group, width).transpose(1, 0, 2)
    text_grad = swap(text_rows, "fsdp").reshape(X, ZH, CORE, share, width)
    text_grad = jnp.where(zl < 6, text_grad, text_grad[:, ::-1])
    text_grad = text_grad.transpose(0, 2, 1, 3, 4).reshape(rows, width)
    return (feature_grad, head_grad, text_grad)


def solution(mesh):
    placed = (P("dp", "fsdp"), P("fsdp", None), P("dp", "fsdp"), P("dp"), P(), P())
    return jax.shard_map(
        on_device,
        mesh=mesh,
        in_specs=placed,
        out_specs=(P("dp", "fsdp"), P("fsdp", None), P("dp", "fsdp")),
        check_vma=False,
    )
```

```python
import jax
import jax.numpy as jnp
from jax import lax
from jax.sharding import PartitionSpec as P

F32, BF16 = jnp.float32, jnp.bfloat16
X, ZH, CORE = 4, 2, 2
ZL, Y = 8, 4
PLANE = [[x * 4 + zh * 2 + c for x in range(X) for c in range(CORE)] for zh in range(ZH)]
RING = [[z * Y + y for y in range(Y)] for z in range(ZL)]
PAIR = [(i, i ^ 2) for i in range(16)]
QUAD = [[(q * 4 + i) * Y + y for i in range(4)] for q in range(ZL // 4) for y in range(Y)]
SLAB = [[(q * 4 + i) * Y + y for y in range(Y) for i in range(4)] for q in range(ZL // 4)]
ACROSS = [(i, i ^ (4 * Y)) for i in range(ZL * Y)]


def place(z, y, x, c):
    return ((z % ZL * Y + y) * X + x) * 4 + z % 16 // ZL * 2 + c


def mirror(z):
    edge = z // 4 * 4 if z % 4 < 2 else z // 4 * 4 + 4
    return (2 * edge - 1 - z) % 16


COLUMNS = [(y, x, c) for y in range(Y) for x in range(X) for c in range(CORE)]
MIRROR = [(place(z, *at), place(mirror(z), *at)) for z in range(16) for at in COLUMNS]
FOLD = (0, 2, 4, 6, 7, 5, 3, 1)
LINE = [[place(z0 + p, *at) for p in FOLD] for z0 in (14, 6) for at in COLUMNS]
LINE_ZL = [(6 + p) % ZL for p in FOLD]


def swap(value, axis, groups=None):
    return lax.all_to_all(value, axis, 0, 0, axis_index_groups=groups, tiled=True)


def spread(value, axis, groups, size):
    copies = jnp.broadcast_to(value[None], (size,) + value.shape)
    return swap(copies, axis, groups)


def on_device(image_feats, image_head, text_embed, text_ids, logit_scale, logit_bias):
    rows, width = image_feats.shape
    embed_width = image_head.shape[1]
    cycle = lax.axis_size("dp")
    group = lax.axis_size("fsdp")
    plane = X * CORE
    own = rows // plane
    held = -(-own // 8) * 8
    share = own // ZH
    d = lax.axis_index("dp")
    f = lax.axis_index("fsdp")

    zl, zh = d // Y, f // CORE % ZH
    k = f // 4 * CORE + f % CORE
    z = zh * ZL + zl
    second = (z >= 6) & (z < 14)
    parts = jnp.broadcast_to(text_embed.reshape(X, 1, CORE, own, width), (X, ZH, CORE, own, width))
    text_part = swap(parts.reshape(group, own, width), "fsdp")
    text_vals = text_part.transpose(1, 0, 2).reshape(own, embed_width).astype(F32)
    text_scale = lax.rsqrt(jnp.sum(text_vals * text_vals, axis=1, keepdims=True) + 1e-06)
    text_unit = text_vals * text_scale
    my_ids = lax.dynamic_slice_in_dim(text_ids, k * own, own, 0).reshape(ZH, share)
    marks = jnp.concatenate([my_ids // 128, my_ids % 128], axis=1).astype(BF16)
    piece = -(-share // 8) * 8
    marks = jnp.pad(marks[:, None], ((0, 0), (0, piece - share - 1), (0, embed_width - 2 * share)))
    halves = jnp.concatenate([text_unit.astype(BF16).reshape(ZH, share, embed_width), marks], axis=1)
    text_unit = jnp.where(second, text_unit[share:], text_unit[:share])
    text_scale = jnp.where(second, text_scale[share:], text_scale[:share])
    there = z // 4 * 4 + jnp.arange(4)
    there = ((there >= 6) & (there < 14))[:, None, None]
    blocks = swap(jnp.where(there, halves[1], halves[0]), "dp", QUAD)
    count = 4 * share
    quad = jnp.concatenate([blocks[:, :share].reshape(count, embed_width), blocks[:, share]], axis=0)
    quad = jnp.pad(quad, ((0, 12), (0, 0)))

    feats = jnp.pad(image_feats.reshape(plane, own, width), ((0, 0), (0, held - own), (0, 0)))
    feats = feats.reshape(plane * held, width)
    term = jnp.dot(feats, image_head, preferred_element_type=F32).astype(BF16)
    term, quad = lax.optimization_barrier((term, quad))
    near = lax.all_gather(quad, "dp", axis_index_groups=RING)
    crossed = lax.ppermute(quad, ("dp", "fsdp"), MIRROR)
    half = swap(term.reshape(plane, held, embed_width), "fsdp", PLANE)
    half = jnp.sum(half.astype(F32), axis=0).astype(BF16)

    far = lax.all_gather(crossed, "dp", axis_index_groups=RING)
    embed = half.astype(F32) + lax.ppermute(half, "fsdp", PAIR).astype(F32)
    image_scale = lax.rsqrt(jnp.sum(embed * embed, axis=1, keepdims=True) + 1e-06)
    image_unit = embed * image_scale
    image_low = spread(image_unit.astype(BF16), "fsdp", PLANE, plane).reshape(plane * held, embed_width)
    lines = (near, far)
    text_low = jnp.stack([part[:, :count] for part in lines], axis=1).reshape(cycle * share, embed_width)
    notes = jnp.stack([part[:, count : count + 4, : 2 * share] for part in lines], axis=1).astype(jnp.int32)
    ids = (notes[..., :share] * 128 + notes[..., share:]).reshape(cycle * share)

    partial_value = jnp.einsum("ie,je->ij", image_low, text_low, preferred_element_type=F32)
    logits = logit_scale * partial_value + logit_bias
    row = lax.broadcasted_iota(jnp.int32, (plane, held), 1)
    row_index = d * rows + lax.broadcasted_iota(jnp.int32, (plane, held), 0) * own + row
    row_index = jnp.where(row < own, row_index, -1).reshape(plane * held, 1)
    sign = jnp.where(row_index == ids[None, :], 1.0, -1.0).astype(F32)
    coef = (-sign * jax.nn.sigmoid(-sign * logits) * logit_scale).astype(BF16)
    unit_part = jnp.einsum("ij,je->ie", coef, text_low, preferred_element_type=F32).astype(BF16)
    unit_part, coef = lax.optimization_barrier((unit_part, coef))
    text_acc = jnp.einsum("ij,ie->je", coef, image_low, preferred_element_type=F32).astype(BF16)

    text_acc = lax.psum_scatter(text_acc.reshape(Y, ZL * share, embed_width), "dp", axis_index_groups=RING)
    back = swap(unit_part.reshape(plane, held, embed_width), "fsdp", PLANE)
    back = jnp.sum(back.astype(F32), axis=0).astype(BF16)
    unit_grad = back.astype(F32) + lax.ppermute(back, "fsdp", PAIR).astype(F32)
    image_dot = jnp.sum(image_unit * unit_grad, axis=1, keepdims=True)
    embed_grad = (image_scale * (unit_grad - image_unit * image_dot)).astype(BF16)
    text_acc = text_acc.reshape(2, 4, share, embed_width)
    text_acc = jnp.where(zl < 4, text_acc, text_acc[::-1]).reshape(ZL, share, embed_width).astype(F32)
    text_acc = jnp.stack([text_acc[at] for at in LINE_ZL])
    embed_grad, text_acc = lax.optimization_barrier((embed_grad, text_acc))
    text_acc = lax.psum_scatter(text_acc, ("dp", "fsdp"), axis_index_groups=LINE)
    grads = spread(embed_grad, "fsdp", PLANE, plane).reshape(plane * held, embed_width)
    head_part = jnp.einsum("rw,re->we", feats, grads, preferred_element_type=F32).astype(BF16)
    head_part = head_part.reshape(Y, width // Y, 4, embed_width // 4).transpose(0, 2, 1, 3)
    head_part = head_part.reshape(4 * Y, width // Y, embed_width // 4)
    head_sum = jnp.sum(swap(head_part, "dp", SLAB).astype(F32), axis=0)
    head_sum = lax.reduce_precision(head_sum, 8, 7)
    head_sum = head_sum + lax.ppermute(head_sum.astype(BF16), "dp", ACROSS).astype(F32)
    head_sum, text_acc = lax.optimization_barrier((head_sum.astype(BF16), text_acc))
    head_all = spread(head_sum, "dp", SLAB, 4 * Y).reshape(Y, 4, width // Y, embed_width // 4)
    head_all = head_all.transpose(0, 2, 1, 3).reshape(width, embed_width)
    head_grad = head_all.astype(F32)
    feature_grad = jnp.einsum("re,we->rw", grads, image_head, preferred_element_type=F32).astype(BF16)
    feature_grad = feature_grad.reshape(plane, held, width)[:, :own].reshape(rows, width)

    text_dot = jnp.sum(text_unit * text_acc, axis=1, keepdims=True)
    text_rows = (text_scale * (text_acc - text_unit * text_dot)).astype(BF16)
    text_rows = text_rows.reshape(share, group, width).transpose(1, 0, 2)
    text_grad = swap(text_rows, "fsdp").reshape(X, ZH, CORE, share, width)
    text_grad = jnp.where(zl < 6, text_grad, text_grad[:, ::-1])
    text_grad = text_grad.transpose(0, 2, 1, 3, 4).reshape(rows, width)
    return (feature_grad, head_grad, text_grad)


def solution(mesh):
    placed = (P("dp", "fsdp"), P("fsdp", None), P("dp", "fsdp"), P("dp"), P(), P())
    return jax.shard_map(
        on_device,
        mesh=mesh,
        in_specs=placed,
        out_specs=(P("dp", "fsdp"), P("fsdp", None), P("dp", "fsdp")),
        check_vma=False,
    )
```

```python
import jax
import jax.numpy as jnp
from jax import lax
from jax.sharding import PartitionSpec as P

F32, BF16 = jnp.float32, jnp.bfloat16
X, ZH, CORE = 4, 2, 2
ZL, Y = 8, 4
PLANE = [[x * 4 + zh * 2 + c for x in range(X) for c in range(CORE)] for zh in range(ZH)]
RING = [[z * Y + y for y in range(Y)] for z in range(ZL)]
PAIR = [(i, i ^ 2) for i in range(16)]
QUAD = [[(q * 4 + i) * Y + y for i in range(4)] for q in range(ZL // 4) for y in range(Y)]
SLAB = [[(q * 4 + i) * Y + y for y in range(Y) for i in range(4)] for q in range(ZL // 4)]
ACROSS = [(i, i ^ (4 * Y)) for i in range(ZL * Y)]


def place(z, y, x, c):
    return ((z % ZL * Y + y) * X + x) * 4 + z % 16 // ZL * 2 + c


def mirror(z):
    edge = z // 4 * 4 if z % 4 < 2 else z // 4 * 4 + 4
    return (2 * edge - 1 - z) % 16


COLUMNS = [(y, x, c) for y in range(Y) for x in range(X) for c in range(CORE)]
MIRROR = [(place(z, *at), place(mirror(z), *at)) for z in range(16) for at in COLUMNS]
ORDER = (2, 3, 1, 0)
FOUR = [
    [place(z0 + (q * 4 + i - 6) % ZL, *at) for i in ORDER] for z0 in (14, 6) for q in range(2) for at in COLUMNS
]


def swap(value, axis, groups=None):
    return lax.all_to_all(value, axis, 0, 0, axis_index_groups=groups, tiled=True)


def spread(value, axis, groups, size):
    copies = jnp.broadcast_to(value[None], (size,) + value.shape)
    return swap(copies, axis, groups)


def on_device(image_feats, image_head, text_embed, text_ids, logit_scale, logit_bias):
    rows, width = image_feats.shape
    embed_width = image_head.shape[1]
    cycle = lax.axis_size("dp")
    group = lax.axis_size("fsdp")
    plane = X * CORE
    own = rows // plane
    held = -(-own // 8) * 8
    share = own // ZH
    d = lax.axis_index("dp")
    f = lax.axis_index("fsdp")

    zl, zh = d // Y, f // CORE % ZH
    k = f // 4 * CORE + f % CORE
    z = zh * ZL + zl
    second = (z >= 6) & (z < 14)
    parts = jnp.broadcast_to(text_embed.reshape(X, 1, CORE, own, width), (X, ZH, CORE, own, width))
    text_part = swap(parts.reshape(group, own, width), "fsdp")
    text_vals = text_part.transpose(1, 0, 2).reshape(own, embed_width).astype(F32)
    text_scale = lax.rsqrt(jnp.sum(text_vals * text_vals, axis=1, keepdims=True) + 1e-06)
    text_unit = text_vals * text_scale
    my_ids = lax.dynamic_slice_in_dim(text_ids, k * own, own, 0).reshape(ZH, share)
    marks = jnp.concatenate([my_ids // 128, my_ids % 128], axis=1).astype(BF16)
    piece = -(-share // 8) * 8
    marks = jnp.pad(marks[:, None], ((0, 0), (0, piece - share - 1), (0, embed_width - 2 * share)))
    halves = jnp.concatenate([text_unit.astype(BF16).reshape(ZH, share, embed_width), marks], axis=1)
    text_unit = jnp.where(second, text_unit[share:], text_unit[:share])
    text_scale = jnp.where(second, text_scale[share:], text_scale[:share])
    there = z // 4 * 4 + jnp.arange(4)
    there = ((there >= 6) & (there < 14))[:, None, None]
    blocks = swap(jnp.where(there, halves[1], halves[0]), "dp", QUAD)
    count = 4 * share
    quad = jnp.concatenate([blocks[:, :share].reshape(count, embed_width), blocks[:, share]], axis=0)
    quad = jnp.pad(quad, ((0, 12), (0, 0)))

    feats = jnp.pad(image_feats.reshape(plane, own, width), ((0, 0), (0, held - own), (0, 0)))
    feats = feats.reshape(plane * held, width)
    term = jnp.dot(feats, image_head, preferred_element_type=F32).astype(BF16)
    term, quad = lax.optimization_barrier((term, quad))
    near = lax.all_gather(quad, "dp", axis_index_groups=RING)
    crossed = lax.ppermute(quad, ("dp", "fsdp"), MIRROR)
    half = swap(term.reshape(plane, held, embed_width), "fsdp", PLANE)
    half = jnp.sum(half.astype(F32), axis=0).astype(BF16)

    _, crossed = lax.optimization_barrier((half, crossed))
    far = lax.all_gather(crossed, "dp", axis_index_groups=RING)
    embed = half.astype(F32) + lax.ppermute(half, "fsdp", PAIR).astype(F32)
    image_scale = lax.rsqrt(jnp.sum(embed * embed, axis=1, keepdims=True) + 1e-06)
    image_unit = embed * image_scale
    image_low = spread(image_unit.astype(BF16), "fsdp", PLANE, plane).reshape(plane * held, embed_width)
    lines = (near, far)
    text_low = jnp.stack([part[:, :count] for part in lines], axis=1).reshape(cycle * share, embed_width)
    notes = jnp.stack([part[:, count : count + 4, : 2 * share] for part in lines], axis=1).astype(jnp.int32)
    ids = (notes[..., :share] * 128 + notes[..., share:]).reshape(cycle * share)

    partial_value = jnp.einsum("ie,je->ij", image_low, text_low, preferred_element_type=F32)
    logits = logit_scale * partial_value + logit_bias
    row = lax.broadcasted_iota(jnp.int32, (plane, held), 1)
    row_index = d * rows + lax.broadcasted_iota(jnp.int32, (plane, held), 0) * own + row
    row_index = jnp.where(row < own, row_index, -1).reshape(plane * held, 1)
    sign = jnp.where(row_index == ids[None, :], 1.0, -1.0).astype(F32)
    coef = (-sign * jax.nn.sigmoid(-sign * logits) * logit_scale).astype(BF16)
    unit_part = jnp.einsum("ij,je->ie", coef, text_low, preferred_element_type=F32).astype(BF16)
    unit_part, coef = lax.optimization_barrier((unit_part, coef))
    text_acc = jnp.einsum("ij,ie->je", coef, image_low, preferred_element_type=F32).astype(BF16)

    text_acc = lax.psum_scatter(text_acc.reshape(Y, ZL * share, embed_width), "dp", axis_index_groups=RING)
    back = swap(unit_part.reshape(plane, held, embed_width), "fsdp", PLANE)
    back = jnp.sum(back.astype(F32), axis=0).astype(BF16)
    unit_grad = back.astype(F32) + lax.ppermute(back, "fsdp", PAIR).astype(F32)
    image_dot = jnp.sum(image_unit * unit_grad, axis=1, keepdims=True)
    embed_grad = (image_scale * (unit_grad - image_unit * image_dot)).astype(BF16)
    text_acc = text_acc.reshape(2, count, embed_width)
    embed_grad, text_acc = lax.optimization_barrier((embed_grad, text_acc))
    crossed = lax.ppermute(text_acc[1], ("dp", "fsdp"), MIRROR)
    grads = spread(embed_grad, "fsdp", PLANE, plane).reshape(plane * held, embed_width)
    text_acc = (text_acc[0].astype(F32) + crossed.astype(F32)).astype(BF16).reshape(4, share, embed_width)
    text_acc = jnp.stack([text_acc[i] for i in ORDER])
    text_acc = lax.psum_scatter(text_acc, ("dp", "fsdp"), axis_index_groups=FOUR)
    head_part = jnp.einsum("rw,re->we", feats, grads, preferred_element_type=F32).astype(BF16)
    head_part = head_part.reshape(Y, width // Y, 4, embed_width // 4).transpose(0, 2, 1, 3)
    head_part = head_part.reshape(4 * Y, width // Y, embed_width // 4)
    head_sum = jnp.sum(swap(head_part, "dp", SLAB).astype(F32), axis=0)
    head_sum = lax.reduce_precision(head_sum, 8, 7)
    head_sum = head_sum + lax.ppermute(head_sum.astype(BF16), "dp", ACROSS).astype(F32)
    head_sum, text_acc = lax.optimization_barrier((head_sum.astype(BF16), text_acc))
    head_all = spread(head_sum, "dp", SLAB, 4 * Y).reshape(Y, 4, width // Y, embed_width // 4)
    head_all = head_all.transpose(0, 2, 1, 3).reshape(width, embed_width)
    head_grad = head_all.astype(F32)
    feature_grad = jnp.einsum("re,we->rw", grads, image_head, preferred_element_type=F32).astype(BF16)
    feature_grad = feature_grad.reshape(plane, held, width)[:, :own].reshape(rows, width)

    text_acc = text_acc.astype(F32)
    text_dot = jnp.sum(text_unit * text_acc, axis=1, keepdims=True)
    text_rows = (text_scale * (text_acc - text_unit * text_dot)).astype(BF16)
    text_rows = text_rows.reshape(share, group, width).transpose(1, 0, 2)
    text_grad = swap(text_rows, "fsdp").reshape(X, ZH, CORE, share, width)
    text_grad = jnp.where(zl < 6, text_grad, text_grad[:, ::-1])
    text_grad = text_grad.transpose(0, 2, 1, 3, 4).reshape(rows, width)
    return (feature_grad, head_grad, text_grad)


def solution(mesh):
    placed = (P("dp", "fsdp"), P("fsdp", None), P("dp", "fsdp"), P("dp"), P(), P())
    return jax.shard_map(
        on_device,
        mesh=mesh,
        in_specs=placed,
        out_specs=(P("dp", "fsdp"), P("fsdp", None), P("dp", "fsdp")),
        check_vma=False,
    )
```

```python
import jax
import jax.numpy as jnp
from jax import lax
from jax.sharding import PartitionSpec as P

F32, BF16 = jnp.float32, jnp.bfloat16
X, ZH, CORE = 4, 2, 2
ZL, Y = 8, 4
PLANE = [[x * 4 + zh * 2 + c for x in range(X) for c in range(CORE)] for zh in range(ZH)]
RING = [[z * Y + y for y in range(Y)] for z in range(ZL)]
SLAB = [[(q * 4 + i) * Y + y for y in range(Y) for i in range(4)] for q in range(ZL // 4)]
ACROSS = [(i, i ^ (4 * Y)) for i in range(ZL * Y)]


def place(z, y, x, c):
    return ((z % ZL * Y + y) * X + x) * 4 + z % 16 // ZL * 2 + c


def mirror(z):
    edge = z // 4 * 4 if z % 4 < 2 else z // 4 * 4 + 4
    return (2 * edge - 1 - z) % 16


COLUMNS = [(y, x, c) for y in range(Y) for x in range(X) for c in range(CORE)]
MIRROR = [(place(z, *at), place(mirror(z), *at)) for z in range(16) for at in COLUMNS]
UP = [(place(z, *at), place(z + 4, *at)) for z in range(16) for at in COLUMNS]
DOWN = [(place(z, *at), place(z - 4, *at)) for z in range(16) for at in COLUMNS]


def across(by):
    def there(z):
        z0 = 6 if 6 <= z < 14 else 14
        return z0 + (z % ZL ^ by) - 6 if (z % ZL ^ by) >= 6 else z0 + (z % ZL ^ by) + 2

    return [(place(z, *at), place(there(z), *at)) for z in range(16) for at in COLUMNS]


def send(value, pairs):
    return lax.ppermute(value, ("dp", "fsdp"), pairs)


def pick(at, parts):
    return jnp.where(at < 2, jnp.where(at == 0, parts[0], parts[1]), jnp.where(at == 2, parts[2], parts[3]))


def swap(value, axis, groups=None):
    return lax.all_to_all(value, axis, 0, 0, axis_index_groups=groups, tiled=True)


def spread(value, axis, groups, size):
    copies = jnp.broadcast_to(value[None], (size,) + value.shape)
    return swap(copies, axis, groups)


def on_device(image_feats, image_head, text_embed, text_ids, logit_scale, logit_bias):
    rows, width = image_feats.shape
    embed_width = image_head.shape[1]
    cycle = lax.axis_size("dp")
    group = lax.axis_size("fsdp")
    plane = X * CORE
    own = rows // plane
    held = -(-own // 8) * 8
    share = own // ZH
    d = lax.axis_index("dp")
    f = lax.axis_index("fsdp")

    zl, zh = d // Y, f // CORE % ZH
    k = f // 4 * CORE + f % CORE
    z = zh * ZL + zl
    second = (z >= 6) & (z < 14)
    parts = jnp.broadcast_to(text_embed.reshape(X, 1, CORE, own, width), (X, ZH, CORE, own, width))
    text_part = swap(parts.reshape(group, own, width), "fsdp")
    text_vals = text_part.transpose(1, 0, 2).reshape(own, embed_width).astype(F32)
    text_scale = lax.rsqrt(jnp.sum(text_vals * text_vals, axis=1, keepdims=True) + 1e-06)
    text_unit = text_vals * text_scale
    my_ids = lax.dynamic_slice_in_dim(text_ids, k * own, own, 0).reshape(ZH, share)
    marks = jnp.concatenate([my_ids // 128, my_ids % 128], axis=1).astype(BF16)
    piece = -(-share // 8) * 8
    marks = jnp.pad(marks[:, None], ((0, 0), (0, piece - share - 1), (0, embed_width - 2 * share)))
    halves = jnp.concatenate([text_unit.astype(BF16).reshape(ZH, share, embed_width), marks], axis=1)
    text_unit = jnp.where(second, text_unit[share:], text_unit[:share])
    text_scale = jnp.where(second, text_scale[share:], text_scale[:share])

    feats = jnp.pad(image_feats.reshape(plane, own, width), ((0, 0), (0, held - own), (0, 0)))
    feats = feats.reshape(plane * held, width)
    term = jnp.dot(feats, image_head, preferred_element_type=F32).astype(BF16)
    term, halves = lax.optimization_barrier((term, halves))

    parts = [jnp.where(second, halves[1], halves[0])]
    for by in (1, 2, 3):
        there = z ^ by
        part = jnp.where((there >= 6) & (there < 14), halves[1], halves[0])
        parts.append(lax.ppermute(part, "dp", [(i, i ^ (by * Y)) for i in range(cycle)]))
    half = swap(term.reshape(plane, held, embed_width), "fsdp", PLANE)
    half = jnp.sum(half.astype(F32), axis=0).astype(BF16)
    half, *parts = lax.optimization_barrier((half, *parts))
    blocks = jnp.stack([pick(z % 4 ^ i, parts) for i in range(4)])
    count = 4 * share
    quad = jnp.concatenate([blocks[:, :share].reshape(count, embed_width), blocks[:, share]], axis=0)
    quad = jnp.pad(quad, ((0, 12), (0, 0)))

    near = lax.all_gather(quad, "dp", axis_index_groups=RING)
    embed = send(half, UP).astype(F32) + send(half, DOWN).astype(F32)
    crossed = send(quad[: count + 8], MIRROR)
    embed, crossed = lax.optimization_barrier((embed, crossed))

    image_scale = lax.rsqrt(jnp.sum(embed * embed, axis=1, keepdims=True) + 1e-06)
    image_unit = embed * image_scale
    image_low = spread(image_unit.astype(BF16), "fsdp", PLANE, plane).reshape(plane * held, embed_width)
    y = d % Y
    far = [crossed] + [lax.ppermute(crossed, "dp", [(i, i ^ by) for i in range(cycle)]) for by in (1, 2, 3)]
    far = jnp.stack([pick(y ^ i, far) for i in range(Y)])
    lines = (near, far)
    text_low = jnp.stack([part[:, :count] for part in lines], axis=1).reshape(cycle * share, embed_width)
    notes = jnp.stack([part[:, count : count + 4, : 2 * share] for part in lines], axis=1).astype(jnp.int32)
    ids = (notes[..., :share] * 128 + notes[..., share:]).reshape(cycle * share)

    partial_value = jnp.einsum("ie,je->ij", image_low, text_low, preferred_element_type=F32)
    logits = logit_scale * partial_value + logit_bias
    row = lax.broadcasted_iota(jnp.int32, (plane, held), 1)
    row_index = (d ^ (4 * Y)) * rows + lax.broadcasted_iota(jnp.int32, (plane, held), 0) * own + row
    row_index = jnp.where(row < own, row_index, -1).reshape(plane * held, 1)
    sign = jnp.where(row_index == ids[None, :], 1.0, -1.0).astype(F32)
    coef = (-sign * jax.nn.sigmoid(-sign * logits) * logit_scale).astype(BF16)
    unit_part = jnp.einsum("ij,je->ie", coef, text_low, preferred_element_type=F32).astype(BF16)
    unit_part, coef = lax.optimization_barrier((unit_part, coef))
    text_acc = jnp.einsum("ij,ie->je", coef, image_low, preferred_element_type=F32).astype(BF16)

    text_acc = lax.psum_scatter(text_acc.reshape(Y, ZL * share, embed_width), "dp", axis_index_groups=RING)
    back = swap(unit_part.reshape(plane, held, embed_width), "fsdp", PLANE)
    unit_grad = jnp.sum(back.astype(F32), axis=0)
    image_dot = jnp.sum(image_unit * unit_grad, axis=1, keepdims=True)
    embed_grad = (image_scale * (unit_grad - image_unit * image_dot)).astype(BF16)
    embed_grad = (send(embed_grad, UP).astype(F32) + send(embed_grad, DOWN).astype(F32)).astype(BF16)
    text_acc = text_acc.reshape(2, count, embed_width)
    embed_grad, text_acc = lax.optimization_barrier((embed_grad, text_acc))
    crossed = send(text_acc[1], MIRROR)
    grads = spread(embed_grad, "fsdp", PLANE, plane).reshape(plane * held, embed_width)
    grads, crossed = lax.optimization_barrier((grads, crossed))
    text_acc = (text_acc[0].astype(F32) + crossed.astype(F32)).reshape(4, share, embed_width)
    i = z % 4
    parts = [send(pick(i ^ by, text_acc).astype(BF16), across(by)) for by in (1, 2, 3)]
    head_part = jnp.einsum("rw,re->we", feats, grads, preferred_element_type=F32).astype(BF16)
    head_part = head_part.reshape(Y, width // Y, 4, embed_width // 4).transpose(0, 2, 1, 3)
    head_part = head_part.reshape(4 * Y, width // Y, embed_width // 4)
    head_sum = jnp.sum(swap(head_part, "dp", SLAB).astype(F32), axis=0)
    head_sum, *parts = lax.optimization_barrier((head_sum, *parts))
    head_sum = lax.reduce_precision(head_sum, 8, 7)
    head_sum = head_sum + lax.ppermute(head_sum.astype(BF16), "dp", ACROSS).astype(F32)
    text_acc = pick(i, text_acc)
    for part in parts:
        text_acc = text_acc + part.astype(F32)
    text_dot = jnp.sum(text_unit * text_acc, axis=1, keepdims=True)
    text_rows = (text_scale * (text_acc - text_unit * text_dot)).astype(BF16)
    text_rows = text_rows.reshape(share, group, width).transpose(1, 0, 2)
    text_grad = swap(text_rows, "fsdp")
    text_grad, head_sum = lax.optimization_barrier((text_grad, head_sum))
    text_grad = text_grad.reshape(X, ZH, CORE, share, width)
    text_grad = jnp.where(zl < 6, text_grad, text_grad[:, ::-1])
    text_grad = text_grad.transpose(0, 2, 1, 3, 4).reshape(rows, width)

    head_all = spread(head_sum.astype(BF16), "dp", SLAB, 4 * Y).reshape(Y, 4, width // Y, embed_width // 4)
    head_all = head_all.transpose(0, 2, 1, 3).reshape(width, embed_width)
    head_grad = head_all.astype(F32)
    feature_grad = jnp.einsum("re,we->rw", grads, image_head, preferred_element_type=F32).astype(BF16)
    feature_grad = feature_grad.reshape(plane, held, width)[:, :own].reshape(rows, width)
    return (feature_grad, head_grad, text_grad)


def solution(mesh):
    placed = (P("dp", "fsdp"), P("fsdp", None), P("dp", "fsdp"), P("dp"), P(), P())
    return jax.shard_map(
        on_device,
        mesh=mesh,
        in_specs=placed,
        out_specs=(P("dp", "fsdp"), P("fsdp", None), P("dp", "fsdp")),
        check_vma=False,
    )
```

```python
import jax
import jax.numpy as jnp
from jax import lax
from jax.sharding import PartitionSpec as P

F32, BF16 = jnp.float32, jnp.bfloat16
X, ZH, CORE = 4, 2, 2
ZL, Y = 8, 4
PLANE = [[x * 4 + zh * 2 + c for x in range(X) for c in range(CORE)] for zh in range(ZH)]
RING = [[z * Y + y for y in range(Y)] for z in range(ZL)]
SLAB = [[(q * 4 + i) * Y + y for y in range(Y) for i in range(4)] for q in range(ZL // 4)]
ACROSS = [(i, i ^ (4 * Y)) for i in range(ZL * Y)]


def place(z, y, x, c):
    return ((z % ZL * Y + y) * X + x) * 4 + z % 16 // ZL * 2 + c


def mirror(z):
    edge = z // 4 * 4 if z % 4 < 2 else z // 4 * 4 + 4
    return (2 * edge - 1 - z) % 16


COLUMNS = [(y, x, c) for y in range(Y) for x in range(X) for c in range(CORE)]
MIRROR = [(place(z, *at), place(mirror(z), *at)) for z in range(16) for at in COLUMNS]
UP = [(place(z, *at), place(z + 4, *at)) for z in range(16) for at in COLUMNS]
DOWN = [(place(z, *at), place(z - 4, *at)) for z in range(16) for at in COLUMNS]


def across(by):
    def there(z):
        z0 = 6 if 6 <= z < 14 else 14
        return z0 + (z % ZL ^ by) - 6 if (z % ZL ^ by) >= 6 else z0 + (z % ZL ^ by) + 2

    return [(place(z, *at), place(there(z), *at)) for z in range(16) for at in COLUMNS]


def send(value, pairs):
    return lax.ppermute(value, ("dp", "fsdp"), pairs)


def pick(at, parts):
    return jnp.where(at < 2, jnp.where(at == 0, parts[0], parts[1]), jnp.where(at == 2, parts[2], parts[3]))


def swap(value, axis, groups=None):
    return lax.all_to_all(value, axis, 0, 0, axis_index_groups=groups, tiled=True)


def spread(value, axis, groups, size):
    copies = jnp.broadcast_to(value[None], (size,) + value.shape)
    return swap(copies, axis, groups)


def on_device(image_feats, image_head, text_embed, text_ids, logit_scale, logit_bias):
    rows, width = image_feats.shape
    embed_width = image_head.shape[1]
    cycle = lax.axis_size("dp")
    plane = X * CORE
    own = rows // plane
    held = -(-own // 8) * 8
    share = own // ZH
    d = lax.axis_index("dp")
    f = lax.axis_index("fsdp")

    zl, zh = d // Y, f // CORE % ZH
    z = zh * ZL + zl
    second = (z >= 6) & (z < 14)
    above = (z + 4) % 16 // ZL == 1

    raw = jnp.stack([text_ids // 128, text_ids % 128], axis=1).astype(BF16)
    raw = jnp.concatenate([text_embed, raw], axis=1)
    up, down = send(raw, UP), send(raw, DOWN)
    raw = jnp.where(above, jnp.concatenate([up[:, :width], down], axis=1), jnp.concatenate([down[:, :width], up], axis=1))
    raw = jnp.pad(raw.reshape(plane, own, -1), ((0, 0), (0, held - own), (0, 0))).reshape(plane * held, -1)
    feats = jnp.pad(image_feats.reshape(plane, own, width), ((0, 0), (0, held - own), (0, 0)))
    feats = feats.reshape(plane * held, width)
    wide = jnp.pad(image_head, ((0, 0), (0, raw.shape[1])))
    term = jnp.dot(feats, wide, preferred_element_type=F32).astype(BF16)
    term = lax.dynamic_update_slice(term, raw, (0, embed_width))
    came = swap(term.reshape(plane, held, -1), "fsdp", PLANE)
    half = jnp.sum(came[:, :, :embed_width].astype(F32), axis=0).astype(BF16)

    text_part = came[:, :own, embed_width : embed_width + ZH * width].reshape(X, CORE, own, ZH, width)
    text_vals = text_part.transpose(2, 0, 3, 1, 4).reshape(own, embed_width).astype(F32)
    text_scale = lax.rsqrt(jnp.sum(text_vals * text_vals, axis=1, keepdims=True) + 1e-06)
    text_unit = text_vals * text_scale
    marks = came[0, :own, embed_width + ZH * width :].reshape(ZH, share, 2)
    marks = marks.transpose(0, 2, 1).reshape(ZH, 2 * share)
    piece = -(-share // 8) * 8
    marks = jnp.pad(marks[:, None], ((0, 0), (0, piece - share - 1), (0, embed_width - 2 * share)))
    halves = jnp.concatenate([text_unit.astype(BF16).reshape(ZH, share, embed_width), marks], axis=1)
    text_unit = jnp.where(second, text_unit[share:], text_unit[:share])
    text_scale = jnp.where(second, text_scale[share:], text_scale[:share])

    parts = [jnp.where(second, halves[1], halves[0])]
    for by in (1, 2, 3):
        there = z ^ by
        part = jnp.where((there >= 6) & (there < 14), halves[1], halves[0])
        parts.append(lax.ppermute(part, "dp", [(i, i ^ (by * Y)) for i in range(cycle)]))
    blocks = jnp.stack([pick(z % 4 ^ i, parts) for i in range(4)])
    count = 4 * share
    quad = jnp.concatenate([blocks[:, :share].reshape(count, embed_width), blocks[:, share]], axis=0)
    quad = jnp.pad(quad, ((0, 12), (0, 0)))

    near = lax.all_gather(quad, "dp", axis_index_groups=RING)
    embed = send(half, UP).astype(F32) + send(half, DOWN).astype(F32)
    crossed = send(quad[: count + 8], MIRROR)

    image_scale = lax.rsqrt(jnp.sum(embed * embed, axis=1, keepdims=True) + 1e-06)
    image_unit = embed * image_scale
    image_low = spread(image_unit.astype(BF16), "fsdp", PLANE, plane).reshape(plane * held, embed_width)
    y = d % Y
    far = [lax.ppermute(crossed, "dp", [(i, i ^ by) for i in range(cycle)]) for by in (1, 3)]
    image_low, last = lax.optimization_barrier((image_low, crossed))
    last = lax.ppermute(last, "dp", [(i, i ^ 2) for i in range(cycle)])
    far = [crossed, far[0], last, far[1]]
    far = jnp.stack([pick(y ^ i, far) for i in range(Y)])
    lines = (near, far)
    text_low = jnp.stack([part[:, :count] for part in lines], axis=1).reshape(cycle * share, embed_width)
    notes = jnp.stack([part[:, count : count + 4, : 2 * share] for part in lines], axis=1).astype(jnp.int32)
    ids = (notes[..., :share] * 128 + notes[..., share:]).reshape(cycle * share)

    partial_value = jnp.einsum("ie,je->ij", image_low, text_low, preferred_element_type=F32)
    logits = logit_scale * partial_value + logit_bias
    row = lax.broadcasted_iota(jnp.int32, (plane, held), 1)
    row_index = (d ^ (4 * Y)) * rows + lax.broadcasted_iota(jnp.int32, (plane, held), 0) * own + row
    row_index = jnp.where(row < own, row_index, -1).reshape(plane * held, 1)
    sign = jnp.where(row_index == ids[None, :], 1.0, -1.0).astype(F32)
    coef = (-sign * jax.nn.sigmoid(-sign * logits) * logit_scale).astype(BF16)
    unit_part = jnp.einsum("ij,je->ie", coef, text_low, preferred_element_type=F32).astype(BF16)
    unit_part, coef = lax.optimization_barrier((unit_part, coef))
    text_acc = jnp.einsum("ij,ie->je", coef, image_low, preferred_element_type=F32).astype(BF16)

    text_acc = lax.psum_scatter(text_acc.reshape(Y, ZL * share, embed_width), "dp", axis_index_groups=RING)
    back = swap(unit_part.reshape(plane, held, embed_width), "fsdp", PLANE)
    unit_grad = jnp.sum(back.astype(F32), axis=0)
    image_dot = jnp.sum(image_unit * unit_grad, axis=1, keepdims=True)
    embed_grad = (image_scale * (unit_grad - image_unit * image_dot)).astype(BF16)
    embed_grad = (send(embed_grad, UP).astype(F32) + send(embed_grad, DOWN).astype(F32)).astype(BF16)
    text_acc = text_acc.reshape(2, count, embed_width)
    embed_grad, text_acc = lax.optimization_barrier((embed_grad, text_acc))
    crossed = send(text_acc[1], MIRROR)
    grads = spread(embed_grad, "fsdp", PLANE, plane).reshape(plane * held, embed_width)
    grads, crossed = lax.optimization_barrier((grads, crossed))
    text_acc = (text_acc[0].astype(F32) + crossed.astype(F32)).reshape(4, share, embed_width)
    i = z % 4
    parts = [send(pick(i ^ by, text_acc).astype(BF16), across(by)) for by in (1, 2, 3)]
    head_part = jnp.einsum("rw,re->we", feats, grads, preferred_element_type=F32).astype(BF16)
    head_part = head_part.reshape(Y, width // Y, 4, embed_width // 4).transpose(0, 2, 1, 3)
    head_part = head_part.reshape(4 * Y, width // Y, embed_width // 4)
    head_sum = jnp.sum(swap(head_part, "dp", SLAB).astype(F32), axis=0)
    head_sum, *parts = lax.optimization_barrier((head_sum, *parts))
    head_sum = lax.reduce_precision(head_sum, 8, 7)
    head_sum = head_sum + lax.ppermute(head_sum.astype(BF16), "dp", ACROSS).astype(F32)
    head_all = spread(head_sum.astype(BF16), "dp", SLAB, 4 * Y)

    text_acc = pick(i, text_acc)
    for part in parts:
        text_acc = text_acc + part.astype(F32)
    text_dot = jnp.sum(text_unit * text_acc, axis=1, keepdims=True)
    text_rows = (text_scale * (text_acc - text_unit * text_dot)).astype(BF16)
    text_rows = text_rows.reshape(share, X, ZH, CORE, width).transpose(2, 1, 3, 0, 4)
    text_rows = text_rows.reshape(ZH, plane, share, width)
    up = send(jnp.where(above, text_rows[1], text_rows[0]), UP)
    down = send(jnp.where(above, text_rows[0], text_rows[1]), DOWN)
    below = (z + 12) % 16
    below = (below >= 6) & (below < 14)
    text_grad = jnp.where(below, jnp.stack([down, up], axis=1), jnp.stack([up, down], axis=1))
    text_grad, head_all = lax.optimization_barrier((text_grad.reshape(plane, own, width), head_all))
    text_grad = swap(text_grad, "fsdp", PLANE).reshape(rows, width)
    head_all = head_all.reshape(Y, 4, width // Y, embed_width // 4).transpose(0, 2, 1, 3).reshape(width, embed_width)
    head_grad = head_all.astype(F32)
    feature_grad = jnp.einsum("re,we->rw", grads, image_head, preferred_element_type=F32).astype(BF16)
    feature_grad = feature_grad.reshape(plane, held, width)[:, :own].reshape(rows, width)
    return (feature_grad, head_grad, text_grad)


def solution(mesh):
    placed = (P("dp", "fsdp"), P("fsdp", None), P("dp", "fsdp"), P("dp"), P(), P())
    return jax.shard_map(
        on_device,
        mesh=mesh,
        in_specs=placed,
        out_specs=(P("dp", "fsdp"), P("fsdp", None), P("dp", "fsdp")),
        check_vma=False,
    )
```

```python
import jax
import jax.numpy as jnp
from jax import lax
from jax.sharding import PartitionSpec as P

F32, BF16 = jnp.float32, jnp.bfloat16
X, ZH, CORE = 4, 2, 2
ZL, Y = 8, 4
PLANE = [[x * 4 + zh * 2 + c for x in range(X) for c in range(CORE)] for zh in range(ZH)]
RING = [[z * Y + y for y in range(Y)] for z in range(ZL)]
PAIR = [(i, i ^ 2) for i in range(16)]
SLAB = [[(q * 4 + i) * Y + y for y in range(Y) for i in range(4)] for q in range(ZL // 4)]
ACROSS = [(i, i ^ (4 * Y)) for i in range(ZL * Y)]


def place(z, y, x, c):
    return ((z % ZL * Y + y) * X + x) * 4 + z % 16 // ZL * 2 + c


def mirror(z):
    edge = z // 4 * 4 if z % 4 < 2 else z // 4 * 4 + 4
    return (2 * edge - 1 - z) % 16


COLUMNS = [(y, x, c) for y in range(Y) for x in range(X) for c in range(CORE)]
MIRROR = [(place(z, *at), place(mirror(z), *at)) for z in range(16) for at in COLUMNS]
FOUR_UP = [(place(z, y, x, c), place(z + 4 - 8 * c, y, x, c)) for z in range(16) for y, x, c in COLUMNS]
FOUR_DOWN = [(place(z, y, x, c), place(z - 4 + 8 * c, y, x, c)) for z in range(16) for y, x, c in COLUMNS]


def across(by):
    def there(z):
        z0 = 6 if 6 <= z < 14 else 14
        return z0 + (z % ZL ^ by) - 6 if (z % ZL ^ by) >= 6 else z0 + (z % ZL ^ by) + 2

    return [(place(z, *at), place(there(z), *at)) for z in range(16) for at in COLUMNS]


def send(value, pairs):
    return lax.ppermute(value, ("dp", "fsdp"), pairs)


def pick(at, parts):
    return jnp.where(at < 2, jnp.where(at == 0, parts[0], parts[1]), jnp.where(at == 2, parts[2], parts[3]))


def swap(value, axis, groups=None):
    return lax.all_to_all(value, axis, 0, 0, axis_index_groups=groups, tiled=True)


def spread(value, axis, groups, size):
    copies = jnp.broadcast_to(value[None], (size,) + value.shape)
    return swap(copies, axis, groups)


def on_device(image_feats, image_head, text_embed, text_ids, logit_scale, logit_bias):
    rows, width = image_feats.shape
    embed_width = image_head.shape[1]
    cycle = lax.axis_size("dp")
    group = lax.axis_size("fsdp")
    plane = X * CORE
    own = rows // plane
    held = -(-own // 8) * 8
    share = own // ZH
    d = lax.axis_index("dp")
    f = lax.axis_index("fsdp")

    zl, zh = d // Y, f // CORE % ZH
    k = f // 4 * CORE + f % CORE
    z = zh * ZL + zl
    second = (z >= 6) & (z < 14)
    parts = jnp.broadcast_to(text_embed.reshape(X, 1, CORE, own, width), (X, ZH, CORE, own, width))
    text_part = swap(parts.reshape(group, own, width), "fsdp")
    text_vals = text_part.transpose(1, 0, 2).reshape(own, embed_width).astype(F32)
    text_scale = lax.rsqrt(jnp.sum(text_vals * text_vals, axis=1, keepdims=True) + 1e-06)
    text_unit = text_vals * text_scale
    my_ids = lax.dynamic_slice_in_dim(text_ids, k * own, own, 0).reshape(ZH, share)
    marks = jnp.concatenate([my_ids // 128, my_ids % 128], axis=1).astype(BF16)
    piece = -(-share // 8) * 8
    marks = jnp.pad(marks[:, None], ((0, 0), (0, piece - share - 1), (0, embed_width - 2 * share)))
    halves = jnp.concatenate([text_unit.astype(BF16).reshape(ZH, share, embed_width), marks], axis=1)
    text_unit = jnp.where(second, text_unit[share:], text_unit[:share])
    text_scale = jnp.where(second, text_scale[share:], text_scale[:share])

    feats = jnp.pad(image_feats.reshape(plane, own, width), ((0, 0), (0, held - own), (0, 0)))
    feats = feats.reshape(plane * held, width)
    term = jnp.dot(feats, image_head, preferred_element_type=F32).astype(BF16)
    term, halves = lax.optimization_barrier((term, halves))

    parts = [jnp.where(second, halves[1], halves[0])]
    for by in (1, 2, 3):
        there = z ^ by
        part = jnp.where((there >= 6) & (there < 14), halves[1], halves[0])
        parts.append(lax.ppermute(part, "dp", [(i, i ^ (by * Y)) for i in range(cycle)]))
    half = swap(term.reshape(plane, held, embed_width), "fsdp", PLANE)
    half = jnp.sum(half.astype(F32), axis=0).astype(BF16)
    half, *parts = lax.optimization_barrier((half, *parts))
    blocks = jnp.stack([pick(z % 4 ^ i, parts) for i in range(4)])
    count = 4 * share
    quad = jnp.concatenate([blocks[:, :share].reshape(count, embed_width), blocks[:, share]], axis=0)
    quad = jnp.pad(quad, ((0, 12), (0, 0)))


    near = lax.all_gather(quad, "dp", axis_index_groups=RING)
    embed = send(half, FOUR_UP).astype(F32) + send(half, FOUR_DOWN).astype(F32)
    crossed = send(quad[: count + 8], MIRROR)

    image_scale = lax.rsqrt(jnp.sum(embed * embed, axis=1, keepdims=True) + 1e-06)
    image_unit = embed * image_scale
    image_low = spread(image_unit.astype(BF16), "fsdp", PLANE, plane).reshape(plane * held, embed_width)
    y = d % Y
    far = [crossed] + [lax.ppermute(crossed, "dp", [(i, i ^ by) for i in range(cycle)]) for by in (1, 2, 3)]
    far = jnp.stack([pick(y ^ i, far) for i in range(Y)])

    row = lax.broadcasted_iota(jnp.int32, (plane, held), 1)
    row_index = (d ^ (4 * Y)) * rows + lax.broadcasted_iota(jnp.int32, (plane, held), 0) * own + row
    row_index = jnp.where(row < own, row_index, -1).reshape(plane * held, 1)
    unit_part, text_acc = 0.0, []
    for part in (near, far):
        texts = part[:, :count].reshape(Y * count, embed_width)
        notes = part[:, count : count + 4, : 2 * share].astype(jnp.int32)
        ids = (notes[..., :share] * 128 + notes[..., share:]).reshape(Y * count)
        partial_value = jnp.einsum("ie,je->ij", image_low, texts, preferred_element_type=F32)
        logits = logit_scale * partial_value + logit_bias
        sign = jnp.where(row_index == ids[None, :], 1.0, -1.0).astype(F32)
        coef = (-sign * jax.nn.sigmoid(-sign * logits) * logit_scale).astype(BF16)
        coef, image_low = lax.optimization_barrier((coef, image_low))
        unit_part = unit_part + jnp.einsum("ij,je->ie", coef, texts, preferred_element_type=F32)
        acc = jnp.einsum("ij,ie->je", coef, image_low, preferred_element_type=F32).astype(BF16)
        text_acc.append(lax.psum_scatter(acc.reshape(Y, count, embed_width), "dp", axis_index_groups=RING))
    unit_part = unit_part.astype(BF16)

    back = swap(unit_part.reshape(plane, held, embed_width), "fsdp", PLANE)
    unit_grad = jnp.sum(back.astype(F32), axis=0)
    image_dot = jnp.sum(image_unit * unit_grad, axis=1, keepdims=True)
    embed_grad = (image_scale * (unit_grad - image_unit * image_dot)).astype(BF16)
    embed_grad = (send(embed_grad, FOUR_UP).astype(F32) + send(embed_grad, FOUR_DOWN).astype(F32)).astype(BF16)
    embed_grad, *text_acc = lax.optimization_barrier((embed_grad, *text_acc))
    crossed = send(text_acc[1], MIRROR)
    grads = spread(embed_grad, "fsdp", PLANE, plane).reshape(plane * held, embed_width)
    grads, crossed = lax.optimization_barrier((grads, crossed))
    text_acc = (text_acc[0].astype(F32) + crossed.astype(F32)).reshape(4, share, embed_width)
    i = z % 4
    parts = [send(pick(i ^ by, text_acc).astype(BF16), across(by)) for by in (1, 2, 3)]
    head_part = jnp.einsum("rw,re->we", feats, grads, preferred_element_type=F32).astype(BF16)
    head_part = head_part.reshape(Y, width // Y, 4, embed_width // 4).transpose(0, 2, 1, 3)
    head_part = head_part.reshape(4 * Y, width // Y, embed_width // 4)
    head_sum = jnp.sum(swap(head_part, "dp", SLAB).astype(F32), axis=0)
    head_sum, *parts = lax.optimization_barrier((head_sum, *parts))
    head_sum = lax.reduce_precision(head_sum, 8, 7)
    head_sum = head_sum + lax.ppermute(head_sum.astype(BF16), "dp", ACROSS).astype(F32)
    head_all = spread(head_sum.astype(BF16), "dp", SLAB, 4 * Y)

    text_acc = pick(i, text_acc)
    for part in parts:
        text_acc = text_acc + part.astype(F32)
    text_dot = jnp.sum(text_unit * text_acc, axis=1, keepdims=True)
    text_rows = (text_scale * (text_acc - text_unit * text_dot)).astype(BF16)
    text_rows = text_rows.reshape(share, X, ZH, CORE, width).transpose(2, 1, 3, 0, 4)
    text_rows = text_rows.reshape(ZH, plane, share, width)
    kept = jnp.where(zh == 0, text_rows[0], text_rows[1])
    came = lax.ppermute(jnp.where(zh == 0, text_rows[1], text_rows[0]), "fsdp", PAIR)
    text_grad = jnp.where(second, jnp.stack([came, kept], axis=1), jnp.stack([kept, came], axis=1))
    text_grad, head_all = lax.optimization_barrier((text_grad.reshape(plane, own, width), head_all))
    text_grad = swap(text_grad, "fsdp", PLANE).reshape(rows, width)
    head_all = head_all.reshape(Y, 4, width // Y, embed_width // 4).transpose(0, 2, 1, 3).reshape(width, embed_width)
    head_grad = head_all.astype(F32)
    feature_grad = jnp.einsum("re,we->rw", grads, image_head, preferred_element_type=F32).astype(BF16)
    feature_grad = feature_grad.reshape(plane, held, width)[:, :own].reshape(rows, width)
    return (feature_grad, head_grad, text_grad)


def solution(mesh):
    placed = (P("dp", "fsdp"), P("fsdp", None), P("dp", "fsdp"), P("dp"), P(), P())
    return jax.shard_map(
        on_device,
        mesh=mesh,
        in_specs=placed,
        out_specs=(P("dp", "fsdp"), P("fsdp", None), P("dp", "fsdp")),
        check_vma=False,
    )
```

```python
import jax
import jax.numpy as jnp
from jax import lax
from jax.sharding import PartitionSpec as P

F32, BF16 = jnp.float32, jnp.bfloat16
X, ZH, CORE = 4, 2, 2
ZL, Y = 8, 4
PLANE = [[x * 4 + zh * 2 + c for x in range(X) for c in range(CORE)] for zh in range(ZH)]
RING = [[z * Y + y for y in range(Y)] for z in range(ZL)]
PAIR = [(i, i ^ 2) for i in range(16)]
SLAB = [[(q * 4 + i) * Y + y for y in range(Y) for i in range(4)] for q in range(ZL // 4)]
ACROSS = [(i, i ^ (4 * Y)) for i in range(ZL * Y)]


def place(z, y, x, c):
    return ((z % ZL * Y + y) * X + x) * 4 + z % 16 // ZL * 2 + c


def mirror(z):
    edge = z // 4 * 4 if z % 4 < 2 else z // 4 * 4 + 4
    return (2 * edge - 1 - z) % 16


COLUMNS = [(y, x, c) for y in range(Y) for x in range(X) for c in range(CORE)]
MIRROR = [(place(z, *at), place(mirror(z), *at)) for z in range(16) for at in COLUMNS]
FOUR_UP = [(place(z, y, x, c), place(z + 4 - 8 * c, y, x, c)) for z in range(16) for y, x, c in COLUMNS]
FOUR_DOWN = [(place(z, y, x, c), place(z - 4 + 8 * c, y, x, c)) for z in range(16) for y, x, c in COLUMNS]


def across(by):
    def there(z):
        z0 = 6 if 6 <= z < 14 else 14
        return z0 + (z % ZL ^ by) - 6 if (z % ZL ^ by) >= 6 else z0 + (z % ZL ^ by) + 2

    return [(place(z, *at), place(there(z), *at)) for z in range(16) for at in COLUMNS]


def send(value, pairs):
    return lax.ppermute(value, ("dp", "fsdp"), pairs)


def pick(at, parts):
    return jnp.where(at < 2, jnp.where(at == 0, parts[0], parts[1]), jnp.where(at == 2, parts[2], parts[3]))


def swap(value, axis, groups=None):
    return lax.all_to_all(value, axis, 0, 0, axis_index_groups=groups, tiled=True)


def spread(value, axis, groups, size):
    copies = jnp.broadcast_to(value[None], (size,) + value.shape)
    return swap(copies, axis, groups)


def on_device(image_feats, image_head, text_embed, text_ids, logit_scale, logit_bias):
    rows, width = image_feats.shape
    embed_width = image_head.shape[1]
    cycle = lax.axis_size("dp")
    group = lax.axis_size("fsdp")
    plane = X * CORE
    own = rows // plane
    held = -(-own // 8) * 8
    share = own // ZH
    d = lax.axis_index("dp")
    f = lax.axis_index("fsdp")

    zl, zh = d // Y, f // CORE % ZH
    k = f // 4 * CORE + f % CORE
    z = zh * ZL + zl
    second = (z >= 6) & (z < 14)
    parts = jnp.broadcast_to(text_embed.reshape(X, 1, CORE, own, width), (X, ZH, CORE, own, width))
    text_part = swap(parts.reshape(group, own, width), "fsdp")
    text_vals = text_part.transpose(1, 0, 2).reshape(own, embed_width).astype(F32)
    text_scale = lax.rsqrt(jnp.sum(text_vals * text_vals, axis=1, keepdims=True) + 1e-06)
    text_unit = text_vals * text_scale
    my_ids = lax.dynamic_slice_in_dim(text_ids, k * own, own, 0).reshape(ZH, share)
    marks = jnp.concatenate([my_ids // 128, my_ids % 128], axis=1).astype(BF16)
    piece = -(-share // 8) * 8
    marks = jnp.pad(marks[:, None], ((0, 0), (0, piece - share - 1), (0, embed_width - 2 * share)))
    halves = jnp.concatenate([text_unit.astype(BF16).reshape(ZH, share, embed_width), marks], axis=1)
    text_unit = jnp.where(second, text_unit[share:], text_unit[:share])
    text_scale = jnp.where(second, text_scale[share:], text_scale[:share])

    feats = jnp.pad(image_feats.reshape(plane, own, width), ((0, 0), (0, held - own), (0, 0)))
    feats = feats.reshape(plane * held, width)
    term = jnp.dot(feats, image_head, preferred_element_type=F32).astype(BF16)
    term, halves = lax.optimization_barrier((term, halves))

    parts = [jnp.where(second, halves[1], halves[0])]
    for by in (1, 2, 3):
        there = z ^ by
        part = jnp.where((there >= 6) & (there < 14), halves[1], halves[0])
        parts.append(lax.ppermute(part, "dp", [(i, i ^ (by * Y)) for i in range(cycle)]))
    half = swap(term.reshape(plane, held, embed_width), "fsdp", PLANE)
    half = jnp.sum(half.astype(F32), axis=0).astype(BF16)
    half, *parts = lax.optimization_barrier((half, *parts))
    blocks = jnp.stack([pick(z % 4 ^ i, parts) for i in range(4)])
    count = 4 * share
    quad = jnp.concatenate([blocks[:, :share].reshape(count, embed_width), blocks[:, share]], axis=0)
    quad = jnp.pad(quad, ((0, 12), (0, 0)))


    near = lax.all_gather(quad, "dp", axis_index_groups=RING)
    embed = send(half, FOUR_UP).astype(F32) + send(half, FOUR_DOWN).astype(F32)
    crossed = send(quad[: count + 8], MIRROR)

    image_scale = lax.rsqrt(jnp.sum(embed * embed, axis=1, keepdims=True) + 1e-06)
    image_unit = embed * image_scale
    image_low = spread(image_unit.astype(BF16), "fsdp", PLANE, plane).reshape(plane * held, embed_width)
    y = d % Y
    far = [crossed] + [lax.ppermute(crossed, "dp", [(i, i ^ by) for i in range(cycle)]) for by in (1, 2, 3)]
    far = jnp.stack([pick(y ^ i, far) for i in range(Y)])

    row = lax.broadcasted_iota(jnp.int32, (plane, held), 1)
    row_index = (d ^ (4 * Y)) * rows + lax.broadcasted_iota(jnp.int32, (plane, held), 0) * own + row
    row_index = jnp.where(row < own, row_index, -1).reshape(plane * held, 1)
    unit_part, text_acc = 0.0, []
    for part in (near, far):
        texts = part[:, :count].reshape(Y * count, embed_width)
        notes = part[:, count : count + 4, : 2 * share].astype(jnp.int32)
        ids = (notes[..., :share] * 128 + notes[..., share:]).reshape(Y * count)
        partial_value = jnp.einsum("ie,je->ij", image_low, texts, preferred_element_type=F32)
        logits = logit_scale * partial_value + logit_bias
        sign = jnp.where(row_index == ids[None, :], 1.0, -1.0).astype(F32)
        coef = (-sign * jax.nn.sigmoid(-sign * logits) * logit_scale).astype(BF16)
        coef, image_low = lax.optimization_barrier((coef, image_low))
        unit_part = unit_part + jnp.einsum("ij,je->ie", coef, texts, preferred_element_type=F32)
        acc = jnp.einsum("ij,ie->je", coef, image_low, preferred_element_type=F32).astype(BF16)
        text_acc.append(lax.psum_scatter(acc.reshape(Y, count, embed_width), "dp", axis_index_groups=RING))
    unit_part = unit_part.astype(BF16)

    back = swap(unit_part.reshape(plane, held, embed_width), "fsdp", PLANE)
    unit_grad = jnp.sum(back.astype(F32), axis=0)
    image_dot = jnp.sum(image_unit * unit_grad, axis=1, keepdims=True)
    embed_grad = (image_scale * (unit_grad - image_unit * image_dot)).astype(BF16)
    embed_grad = (send(embed_grad, FOUR_UP).astype(F32) + send(embed_grad, FOUR_DOWN).astype(F32)).astype(BF16)
    embed_grad, text_acc[1] = lax.optimization_barrier((embed_grad, text_acc[1]))
    crossed = send(text_acc[1], MIRROR)
    grads = spread(embed_grad, "fsdp", PLANE, plane).reshape(plane * held, embed_width)
    grads, crossed = lax.optimization_barrier((grads, crossed))
    text_acc = (text_acc[0].astype(F32) + crossed.astype(F32)).reshape(4, share, embed_width)
    i = z % 4
    parts = [send(pick(i ^ by, text_acc).astype(BF16), across(by)) for by in (1, 2, 3)]
    head_part = jnp.einsum("rw,re->we", feats, grads, preferred_element_type=F32).astype(BF16)
    head_part = head_part.reshape(Y, width // Y, 4, embed_width // 4).transpose(0, 2, 1, 3)
    head_part = head_part.reshape(4 * Y, width // Y, embed_width // 4)
    head_sum = jnp.sum(swap(head_part, "dp", SLAB).astype(F32), axis=0)
    head_sum, *parts = lax.optimization_barrier((head_sum, *parts))
    head_sum = lax.reduce_precision(head_sum, 8, 7)
    head_sum = head_sum + lax.ppermute(head_sum.astype(BF16), "dp", ACROSS).astype(F32)
    head_all = spread(head_sum.astype(BF16), "dp", SLAB, 4 * Y)

    text_acc = pick(i, text_acc)
    for part in parts:
        text_acc = text_acc + part.astype(F32)
    text_dot = jnp.sum(text_unit * text_acc, axis=1, keepdims=True)
    text_rows = (text_scale * (text_acc - text_unit * text_dot)).astype(BF16)
    text_rows = text_rows.reshape(share, X, ZH, CORE, width).transpose(2, 1, 3, 0, 4)
    text_rows = text_rows.reshape(ZH, plane, share, width)
    kept = jnp.where(zh == 0, text_rows[0], text_rows[1])
    came = lax.ppermute(jnp.where(zh == 0, text_rows[1], text_rows[0]), "fsdp", PAIR)
    text_grad = jnp.where(second, jnp.stack([came, kept], axis=1), jnp.stack([kept, came], axis=1))
    text_grad, head_all = lax.optimization_barrier((text_grad.reshape(plane, own, width), head_all))
    text_grad = swap(text_grad, "fsdp", PLANE).reshape(rows, width)
    head_all = head_all.reshape(Y, 4, width // Y, embed_width // 4).transpose(0, 2, 1, 3).reshape(width, embed_width)
    head_grad = head_all.astype(F32)
    feature_grad = jnp.einsum("re,we->rw", grads, image_head, preferred_element_type=F32).astype(BF16)
    feature_grad = feature_grad.reshape(plane, held, width)[:, :own].reshape(rows, width)
    return (feature_grad, head_grad, text_grad)


def solution(mesh):
    placed = (P("dp", "fsdp"), P("fsdp", None), P("dp", "fsdp"), P("dp"), P(), P())
    return jax.shard_map(
        on_device,
        mesh=mesh,
        in_specs=placed,
        out_specs=(P("dp", "fsdp"), P("fsdp", None), P("dp", "fsdp")),
        check_vma=False,
    )
```
